32 devices in a mesh: row: 16 (over z, y, x), col: 2 (over core).
Axes of the slice: x: 2, y: 2, z: 4, core: 2. Of those that a mesh axis runs over, the one named last changes fastest.
Arguments:
- dinv0: bfloat16 [16384, 4096], P('row', 'col'), as said below
- dinv1: bfloat16 [8192, 4096], P('row', 'col'), as said below
- dinv2: bfloat16 [4096, 4096], P('row', 'col'), as said below
- offdiag0: bfloat16 [16384, 4096], P('row', 'col'), may hold values from -0.0625 to 0.0625
- offdiag1: bfloat16 [8192, 4096], P('row', 'col'), may hold values from -0.0625 to 0.0625
- rhs0: bfloat16 [16384, 128], P(('row', 'col')), may hold values from -6 to 6
- rhs1: bfloat16 [8192, 128], P(('row', 'col')), may hold values from -6 to 6
- rhs2: bfloat16 [4096, 128], P(('row', 'col')), may hold values from -6 to 6
- block_rows0: int32 [4, 64, 16], replicated, may hold values from 0 to 63, all different within a row
- block_rows1: int32 [2, 64, 16], replicated, may hold values from 0 to 63, all different within a row
Outputs:
- solution0: float32 [16384, 128], P(('row', 'col'))
- solution1: float32 [8192, 128], P(('row', 'col'))
- solution2: float32 [4096, 128], P(('row', 'col'))
The draws below stay inside these ranges and needn't reach their ends.
Inputs may be any that keep to these rules, and one draw needn't show every extreme that they name: `block_rows0`: each row of the last dimension lists 16 different block rows. `block_rows1`: each row of the last dimension lists 16 different block rows. `dinv0`: each supernode's block is lower triangular in global order, with a positive diagonal. `dinv1`: each supernode's block is lower triangular in global order, with a positive diagonal. `dinv2`: each supernode's block is lower triangular in global order, with a positive diagonal.
All inputs are finite; a program needn't handle non-finite values.
Results may differ from the reference program's by a relative error of at most 0.0095.
Values may be sent and summed in bfloat16 or wider, within the bound.
A program may use at most 64 MiB of HBM per device.

```python
import jax
import jax.numpy as jnp
from jax import lax

SNW = 4096
NRHS = 128
MB = 64
KB = 16
GR = 4
NL0 = 4
NL1 = 2
NL2 = 1
NBLK = 64
CD = 2048
MC = 32
N_COL = 2


def inverse_blocks(key, salt, count, group):
    key_off, key_diag = jax.random.split(jax.random.fold_in(key, salt))
    stored = jnp.arange(SNW, dtype=jnp.int32)
    rows_each = SNW // group
    global_rows = (stored % rows_each // MB * group + stored // rows_each) * MB + stored % MB
    inner = stored % CD
    global_columns = inner // MC * MB + stored // CD * MC + inner % MC
    below = global_rows[:, None] > global_columns[None, :]
    same = global_rows[:, None] == global_columns[None, :]
    lower = 0.7 * jax.random.normal(key_off, (count, SNW, SNW), jnp.float32)
    diag_values = jax.random.uniform(key_diag, (count, SNW), jnp.float32, 0.7, 1.4)
    lower = lower * (1.0 / SNW ** 0.5)
    values = jnp.where(below[None, :, :], lower, jnp.where(same[None, :, :], diag_values[:, :, None], 0.0))
    return values.reshape(count * SNW, SNW).astype(jnp.bfloat16)


def draw_dinv0(key, part):
    return inverse_blocks(key, 11, NL0, GR)


def draw_dinv1(key, part):
    return inverse_blocks(key, 23, NL1, 2 * GR)


def draw_dinv2(key, part):
    return inverse_blocks(key, 37, NL2, 4 * GR)


def block_levels(key, shape, cuts, low, largest):
    gain = 1.0
    for axis_at, blocks in cuts:
        heights = jax.random.uniform(jax.random.fold_in(jax.random.fold_in(key, 6), axis_at), (blocks,), jnp.float32, low / len(cuts), largest / len(cuts))
        gain = gain * jnp.repeat(jnp.exp(heights), shape[axis_at] // blocks).reshape((-1,) + (1,) * (len(shape) - 1 - axis_at))
    return gain


def distinct(key, rows, count, top, lift):
    sequence = jax.random.permutation(jax.random.fold_in(key, 1), count)
    favour = sequence
    for power in range(3):
        favour = favour * favour // count
    favour = favour * lift // count
    chance = jax.random.randint(jax.random.fold_in(key, 2), (rows, count), 0, 4096) + favour
    sure = jax.random.permutation(jax.random.fold_in(key, 3), rows)[jnp.arange(count) % rows]
    chance = jnp.where(jnp.arange(rows)[:, None] == sure[None, :], 1 << 14, chance)
    merit = chance * count + jnp.arange(count)
    return lax.top_k(merit.astype(jnp.int32), top)[1].astype(jnp.int32)


def gaussian(rng, shape, scale, most, pieces=(), held_as=jnp.bfloat16):
    result = scale * jax.random.normal(rng, shape, jnp.float32)
    if pieces:
        result = result * block_levels(rng, shape, pieces, -0.22, 0.18)
    return jnp.clip(result, -most, most).astype(held_as)


def setup_inputs(seed: int = 0) -> dict:
    streams_of = jax.random.split(jax.random.key(seed), 11)
    dinv0 = draw_dinv0(jax.random.fold_in(streams_of[10], 71), 0)
    dinv1 = draw_dinv1(jax.random.fold_in(streams_of[10], 71), 0)
    dinv2 = draw_dinv2(jax.random.fold_in(streams_of[10], 71), 0)
    offdiag0 = gaussian(streams_of[3], (NL0 * SNW, SNW), (2 * SNW) ** -0.5, 0.0625, ((0, 16), (1, 2)))
    offdiag1 = gaussian(streams_of[4], (NL1 * SNW, SNW), (2 * SNW) ** -0.5, 0.0625, ((0, 16), (1, 2)))
    rhs0 = gaussian(streams_of[5], (NL0 * SNW, NRHS), 1.0, 6.0, ((0, 32),))
    rhs1 = gaussian(streams_of[6], (NL1 * SNW, NRHS), 1.0, 6.0, ((0, 32),))
    rhs2 = gaussian(streams_of[7], (NL2 * SNW, NRHS), 1.0, 6.0, ((0, 32),))
    block_rows0 = distinct(streams_of[8], NL0 * NBLK, NBLK, KB, 4096).reshape((NL0, NBLK, KB))
    block_rows1 = distinct(streams_of[9], NL1 * NBLK, NBLK, KB, 4096).reshape((NL1, NBLK, KB))
    return {"dinv0": dinv0, "dinv1": dinv1, "dinv2": dinv2, "offdiag0": offdiag0, "offdiag1": offdiag1, "rhs0": rhs0, "rhs1": rhs1, "rhs2": rhs2, "block_rows0": block_rows0, "block_rows1": block_rows1}


def row_order(group):
    stored = jnp.arange(SNW, dtype=jnp.int32)
    rows_each = SNW // group
    owner = stored // rows_each
    block = (stored % rows_each) // MB
    return (block * group + owner) * MB + stored % MB


def column_order():
    stored = jnp.arange(SNW, dtype=jnp.int32)
    owner = stored // CD
    inner = stored % CD
    return (inner // MC) * MB + owner * MC + inner % MC


def piece_order(group):
    stored = jnp.arange(SNW, dtype=jnp.int32)
    blocks = SNW // (group * MB)
    unit = stored % MC
    rest = stored // MC
    block = rest % blocks
    rest = rest // blocks
    column_dev = rest % N_COL
    row_dev = rest // N_COL
    return ((block * group + row_dev) * N_COL + column_dev) * MC + unit


def to_global(side, order, count):
    shaped = side.reshape(count, SNW, NRHS)
    return jnp.zeros_like(shaped).at[:, order].set(shaped)


def masked(matrix, listing, rows, columns):
    identity = jnp.arange(NBLK, dtype=jnp.int32)
    listed = jnp.any(listing[None, :, :] == identity[:, None, None], axis=-1)
    keep = listed[rows // MB][:, columns // MB]
    return jnp.where(keep, matrix, jnp.zeros_like(matrix))


def apply_plain(matrix, vector, rows, columns):
    stored_out = jnp.dot(matrix, vector[columns], preferred_element_type=jnp.float32)
    return jnp.zeros((SNW, NRHS), jnp.float32).at[rows].set(stored_out)


def apply_transposed(matrix, vector, rows, columns):
    stored_out = jnp.dot(matrix.T, vector[rows], preferred_element_type=jnp.float32)
    return jnp.zeros((SNW, NRHS), jnp.float32).at[columns].set(stored_out)


def reference(dinv0, dinv1, dinv2, offdiag0, offdiag1, rhs0, rhs1, rhs2, block_rows0, block_rows1):
    groups = (GR, 2 * GR, 4 * GR)
    counts = (NL0, NL1, NL2)
    inverses = (dinv0, dinv1, dinv2)
    couplings = (offdiag0, offdiag1)
    listings = (block_rows0, block_rows1)
    sides = (rhs0, rhs1, rhs2)
    columns = column_order()
    solved = []
    update = None
    for level in range(3):
        rows = row_order(groups[level])
        right = to_global(sides[level], piece_order(groups[level]), counts[level]).astype(jnp.float32)
        if update is not None:
            right = right - update
        residual = right.astype(jnp.bfloat16)
        matrices = inverses[level].reshape(counts[level], SNW, SNW)
        solved_level = lax.map(lambda item: apply_plain(item[0], item[1], rows, columns).astype(jnp.bfloat16), (matrices, residual))
        solved.append(solved_level)
        if level < 2:
            coupled = couplings[level].reshape(counts[level], SNW, SNW)
            terms = lax.map(lambda item: apply_plain(masked(item[0], item[2], rows, columns), item[1], rows, columns), (coupled, solved_level, listings[level]))
            update = terms.reshape(counts[level] // 2, 2, SNW, NRHS).sum(axis=1)
    outputs = [None, None, None]
    carried = None
    for level in (2, 1, 0):
        rows = row_order(groups[level])
        total = solved[level].astype(jnp.float32)
        if carried is not None:
            total = total - carried
        weighted = total.astype(jnp.bfloat16)
        matrices = inverses[level].reshape(counts[level], SNW, SNW)
        answer = lax.map(lambda item: apply_transposed(item[0], item[1], rows, columns), (matrices, weighted))
        outputs[level] = answer[:, piece_order(groups[level])].reshape(counts[level] * SNW, NRHS)
        if level > 0:
            rounded = answer.astype(jnp.bfloat16)
            child_rows = row_order(groups[level - 1])
            parent_for_child = jnp.repeat(rounded, 2, axis=0)
            coupled = couplings[level - 1].reshape(counts[level - 1], SNW, SNW)
            carried = lax.map(lambda item: apply_transposed(masked(item[0], item[2], child_rows, columns), item[1], child_rows, columns), (coupled, parent_for_child, listings[level - 1]))
    return (outputs[0], outputs[1], outputs[2])
```

```python
import functools

import jax
import jax.numpy as jnp
from jax import lax
from jax.experimental import pallas as pl
from jax.experimental.pallas import tpu as pltpu
from jax.sharding import PartitionSpec as P

MESH = pl.DeviceIdType.MESH


class Exchange:
    def __init__(self, send_sems, recv_sems, row, col):
        self.send_sems, self.recv_sems = send_sems, recv_sems
        self.row, self.col = row, col
        self.used = 0
        self.sent = []

    def across(self, flips):
        where = self.row
        bit = 1
        while bit <= flips:
            if flips & bit:
                where = where + (1 - 2 * (self.row // bit % 2)) * bit
            bit *= 2
        return where

    def start(self, src, dst, flips=0, other_col=False):
        col = 1 - self.col if other_col else self.col
        copy = pltpu.make_async_remote_copy(
            src_ref=src,
            dst_ref=dst,
            send_sem=self.send_sems.at[self.used],
            recv_sem=self.recv_sems.at[self.used],
            device_id=(self.across(flips), col),
            device_id_type=MESH,
        )
        self.used += 1
        copy.start()
        self.sent.append(copy)
        return copy

    def finish(self):
        for copy in self.sent:
            copy.wait_send()


def solve_kernel(
    groups, blocks, n_cols, mc, width, others,
    dinv0, dinv1, dinv2, off0, off1, rhs0, rhs1, rhs2, list0, list1,
    out0, out1, out2,
    d0, d1, d2, l0, l1, b1, b2, n0, n1, mask,
    gr0, gr1, gr2, gx0, gx1,
    fp0, fp1, fp2, cp0, cp1,
    fr0, fr1, fr2, cr0, cr1,
    su0, su1, sb0, sb1, ub0, ub1,
    rw0, rw1, rw2, kw0, kw1, turned0, turned1, turned2,
    tf0, tf1, tf2, th0, th1, th2, kf0, kf1, kh0, kh1,
    tr0, tr1, tr2, kr0, kr1, zf, zh, zr,
    send_sems, recv_sems, local_sems,
):
    row, col = lax.axis_index("row"), lax.axis_index("col")
    ex = Exchange(send_sems, recv_sems, row, col)
    mb = 2 * mc
    local = [row % g for g in groups]
    plane = groups[0]
    f32, bf16 = jnp.float32, jnp.bfloat16

    member0, member1 = row // groups[0], row // groups[1]
    pairs = [
        (rhs0, gr0.at[:, local[0]]), (dinv0, d0), (list0.at[member0], n0), (off0, l0),
        (list1.at[member1], n1), (dinv1, d1), (off1, l1), (dinv2, d2), (rhs1, b1), (rhs2, b2),
    ]
    loads = []
    for at, (src, dst) in enumerate(pairs):
        loads.append(pltpu.make_async_copy(src, dst, local_sems.at[at]))
        loads[-1].start()

    barrier = pltpu.get_barrier_semaphore()
    for flips in others:
        pl.semaphore_signal(barrier, inc=1, device_id=(ex.across(flips), col), device_id_type=MESH)
    pl.semaphore_signal(barrier, inc=1, device_id=(row, 1 - col), device_id_type=MESH)
    pl.semaphore_wait(barrier, len(others) + 1)

    def gather(buf, level, src=None):
        mine = buf.at[:, local[level]]
        first = mine if src is None else src
        return [ex.start(first, mine, k) for k in range(1, groups[level])]

    def gather_top(buf):
        high = groups[2] // plane
        mine = buf.at[:, local[2]]
        along = [ex.start(mine, mine, s * plane) for s in range(1, high)]
        waits = [ex.start(mine, mine, k) for k in range(1, plane)]
        for s in range(1, high):
            along[s - 1].wait_recv()
            slot = buf.at[:, ex.across(s * plane) % groups[2]]
            waits += [ex.start(slot, slot, k) for k in range(1, plane)]
        return waits

    def received(copies):
        for copy in copies:
            copy.wait_recv()

    def apply_rows(matrix, buf, prod, level):
        count = blocks[level]
        step = min(count, 256 // mb)

        def body(i, carry):
            tile = matrix[pl.ds(i * step * mb, step * mb), :]
            full = buf[...].reshape(n_cols, width)
            res = jnp.dot(tile, full, preferred_element_type=f32)
            prod[pl.ds(i * step, step)] = res.reshape(step, 2, mc, width)
            return carry

        lax.fori_loop(0, count // step, body, 0)

    def col_sum(prod, recv):
        copy = ex.start(prod.at[:, 1 - col], recv, other_col=True)
        copy.wait_recv()
        return prod[:, col] + recv[...]

    def build_mask(matrix, listing, level):
        lanes = lax.broadcasted_iota(jnp.int32, (1, 128), 1)
        owned = lanes * groups[level] + local[level]
        listed = jnp.zeros((listing.shape[0], 128), f32)
        for k in range(listing.shape[1]):
            listed = listed + jnp.where(listing[:, k:k + 1] == owned, 1.0, 0.0)
        unit = lax.broadcasted_iota(jnp.int32, (listing.shape[0], n_cols), 1) // mc
        which = lax.broadcasted_iota(jnp.int32, (listing.shape[0], n_cols), 0)
        spread = jnp.where(unit == which, 1.0, 0.0).astype(bf16)
        mask[...] = lax.dot_general(
            listed.astype(bf16), spread, (((0,), (0,)), ((), ())), preferred_element_type=f32
        )

        def body(i, carry):
            rows = pl.ds(i * mb, mb)
            keep = jnp.broadcast_to(mask[pl.ds(i, 1), :], (mb, n_cols)).astype(bf16)
            matrix[rows, :] = matrix[rows, :] * keep
            return carry

        lax.fori_loop(0, blocks[level], body, 0)

    def apply_turned(matrix, form, turned, prod, half, level):
        count, group = blocks[level], groups[level]
        turned[...] = form.T
        cols = max(256, mc * group)
        step = cols // (mc * group)
        tail = prod.shape[1:]

        def body(i, carry):
            tile = matrix[:, pl.ds(pl.multiple_of(i * cols, cols), cols)]
            res = jnp.dot(turned[...], tile, preferred_element_type=f32)
            res = res.T.reshape((step,) + tail)
            prod[pl.ds(i * step, step)] = res
            half[pl.ds(i * step, step)] = res.astype(bf16)
            return carry

        lax.fori_loop(0, n_cols // cols, body, 0)

    def fold(prod, half, recv, level):
        group = groups[level]
        copies = [
            ex.start(half.at[:, ex.across(k) % group], recv.at[k - 1], k) for k in range(1, group)
        ]
        total = prod[:, local[level]]
        for k, copy in enumerate(copies):
            copy.wait_recv()
            total = total + recv[k].astype(f32)
        return total

    def fold_top(prod, half, recv):
        high = groups[2] // plane
        copies = [
            ex.start(half.at[:, :, ex.across(k) % plane], recv.at[k - 1], k)
            for k in range(1, plane)
        ]
        total = prod[:, :, row % plane]
        for k, copy in enumerate(copies):
            copy.wait_recv()
            total = total + recv[k].astype(f32)
        zf[...] = total
        zh[...] = total.astype(bf16)
        copies = [
            ex.start(zh.at[:, ex.across(s * plane) // plane % high], zr.at[s - 1], s * plane)
            for s in range(1, high)
        ]
        total = zf[:, row // plane % high]
        for s, copy in enumerate(copies):
            copy.wait_recv()
            total = total + zr[s].astype(f32)
        return total

    gathers = (gr0, gr1, gr2)
    solved = (gx0, gx1)
    inverses, couplings, listings = (d0, d1, d2), (l0, l1), (n0, n1)
    sides = (None, b1, b2)

    copies = gather(gr0, 0, rhs0)
    for at in (2, 3, 4, 6):
        loads[at].wait()
    build_mask(l0, n0, 0)
    loads[1].wait()
    loads[0].wait()
    received(copies)
    for level in range(3):
        prod, recv = (fp0, fp1, fp2)[level], (fr0, fr1, fr2)[level]
        apply_rows(inverses[level], gathers[level], prod, level)
        found = col_sum(prod, recv).astype(bf16)
        if level == 2:
            break
        solved[level][:, local[level]] = found
        copies = gather(solved[level], level)
        if level == 0:
            build_mask(l1, n1, 1)
            for at in (5, 7, 8, 9):
                loads[at].wait()
        received(copies)
        prod, recv = (cp0, cp1)[level], (cr0, cr1)[level]
        apply_rows(couplings[level], solved[level], prod, level)
        summed = col_sum(prod, recv).reshape(blocks[level] // 2, 2, mc, width)
        keep, away, landed = (su0, su1)[level], (sb0, sb1)[level], (ub0, ub1)[level]
        keep[...] = summed
        away[...] = summed.astype(bf16)
        side = row // groups[level] % 2
        copy = ex.start(away.at[:, 1 - side], landed, groups[level])
        copy.wait_recv()
        update = keep[:, side] + landed[...].astype(f32)
        residual = (sides[level + 1][...].astype(f32) - update).astype(bf16)
        gathers[level + 1][:, local[level + 1]] = residual
        if level == 0:
            received(gather(gathers[1], 1))
        else:
            received(gather_top(gathers[2]))

    weighted = found
    for level in (2, 1, 0):
        form = (rw0, rw1, rw2)[level]
        turned = (turned0, turned1, turned2)[level]
        form[:, col] = weighted
        copy = ex.start(form.at[:, col], form.at[:, col], other_col=True)
        copy.wait_recv()
        prod, half = (tf0, tf1, tf2)[level], (th0, th1, th2)[level]
        rows = blocks[level] * mb
        apply_turned(inverses[level], form[...].reshape(rows, width), turned, prod, half, level)
        if level == 2:
            answer = fold_top(prod, half, tr2)
        else:
            answer = fold(prod, half, (tr0, tr1)[level], level)
        if level > 0:
            below = level - 1
            child = (kw0, kw1)[below]
            side = row // groups[below] % 2
            child[:, side, col] = answer.astype(bf16)
            mine = child.at[:, side, col]
            away = ex.start(mine, mine, groups[below])
            near = ex.start(mine, mine, other_col=True)
        (out0, out1, out2)[level][...] = answer
        if level > 0:
            away.wait_recv()
            theirs = child.at[:, 1 - side, col]
            far = ex.start(theirs, theirs, other_col=True)
            near.wait_recv()
            far.wait_recv()
            prod, half, recv = (kf0, kf1)[below], (kh0, kh1)[below], (kr0, kr1)[below]
            rows = blocks[below] * mb
            turned = (turned0, turned1)[below]
            apply_turned(
                couplings[below], child[...].reshape(rows, width), turned, prod, half, below
            )
            carried = fold(prod, half, recv, below)
            own = solved[below][:, local[below]].astype(f32)
            weighted = (own - carried).astype(bf16)
    ex.finish()


def fused(args, groups, mc):
    dinv0, dinv1, dinv2, off0, off1, rhs0, rhs1, rhs2, list0, list1 = args
    n_cols = dinv0.shape[1]
    width = rhs0.shape[1]
    mb = 2 * mc
    blocks = [d.shape[0] // mb for d in (dinv0, dinv1, dinv2)]
    high = groups[2] // groups[0]
    others = sorted(set(range(1, groups[1])) | {s * groups[0] for s in range(1, high)} | {groups[1]})
    bf16, f32 = jnp.bfloat16, jnp.float32
    V = pltpu.VMEM
    r0, r1, r2 = blocks
    g0, g1, g2 = groups

    def unit(dtype, *lead):
        return V(lead + (mc, width), dtype)

    scratch = [V(a.shape, bf16) for a in (dinv0, dinv1, dinv2, off0, off1)]
    scratch += [unit(bf16, r1), unit(bf16, r2)]
    scratch += [V(list0.shape[1:], jnp.int32), V(list1.shape[1:], jnp.int32)]
    scratch += [V((128, n_cols), f32)]
    scratch += [unit(bf16, r, g) for r, g in ((r0, g0), (r1, g1), (r2, g2), (r0, g0), (r1, g1))]
    scratch += [unit(f32, r, 2) for r in (r0, r1, r2, r0, r1)]
    scratch += [unit(f32, r) for r in (r0, r1, r2, r0, r1)]
    scratch += [unit(f32, r0 // 2, 2), unit(f32, r1 // 2, 2)]
    scratch += [unit(bf16, r0 // 2, 2), unit(bf16, r1 // 2, 2)]
    scratch += [unit(bf16, r0 // 2), unit(bf16, r1 // 2)]
    scratch += [unit(bf16, r, 2) for r in (r0, r1, r2)]
    scratch += [unit(bf16, r0 // 2, 2, 2), unit(bf16, r1 // 2, 2, 2)]
    scratch += [V((width, r * mb), bf16) for r in blocks]
    top = (r2, high, g0)
    scratch += [unit(f32, r0, g0), unit(f32, r1, g1), unit(f32, *top)]
    scratch += [unit(bf16, r0, g0), unit(bf16, r1, g1), unit(bf16, *top)]
    scratch += [unit(f32, r0, g0), unit(f32, r1, g1)]
    scratch += [unit(bf16, r0, g0), unit(bf16, r1, g1)]
    scratch += [unit(bf16, g0 - 1, r0), unit(bf16, g1 - 1, r1), unit(bf16, g0 - 1, r2, high)]
    scratch += [unit(bf16, g0 - 1, r0), unit(bf16, g1 - 1, r1)]
    scratch += [unit(f32, r2, high), unit(bf16, r2, high), unit(bf16, high - 1, r2)]
    count = 4 * (g0 - 1) + 4 * (g1 - 1) + 5 * high * g0 + 32
    scratch += [pltpu.SemaphoreType.DMA((count,)), pltpu.SemaphoreType.DMA((count,))]
    scratch += [pltpu.SemaphoreType.DMA((10,))]
    macs = sum(d.shape[0] for d in (dinv0, dinv1, dinv2, off0, off1)) * n_cols * width
    outs = pl.pallas_call(
        functools.partial(solve_kernel, groups, blocks, n_cols, mc, width, others),
        out_shape=[jax.ShapeDtypeStruct((r, mc, width), f32) for r in blocks],
        in_specs=[pl.BlockSpec(memory_space=pl.ANY)] * 10,
        out_specs=[pl.BlockSpec(memory_space=pltpu.VMEM)] * 3,
        scratch_shapes=scratch,
        cost_estimate=pl.CostEstimate(
            flops=4 * macs, bytes_accessed=2 * macs // width, transcendentals=0
        ),
        compiler_params=pltpu.CompilerParams(
            collective_id=0, has_side_effects=True, vmem_limit_bytes=56 * 1024 * 1024
        ),
    )(
        dinv0, dinv1, dinv2, off0, off1,
        *[side.reshape(-1, mc, width) for side in (rhs0, rhs1, rhs2)],
        list0, list1,
    )
    return tuple(out.reshape(-1, width) for out in outs)


def partner(value, axis, stride):
    return lax.ppermute(value, axis, [(i, i ^ 1 << stride) for i in range(lax.axis_size(axis))])


def own_bit(which):
    return lax.axis_index("row") >> which & 1


def row_join(pieces, depth):
    joined = pieces
    for which in range(depth):
        other = partner(joined, "row", which)
        first = jnp.concatenate((joined, other), axis=1)
        second = jnp.concatenate((other, joined), axis=1)
        joined = jnp.where(own_bit(which) == 0, first, second)
    return joined.reshape(-1, joined.shape[-1])


def row_fold(partial_value, row_blocks, depth):
    width = partial_value.shape[-1]
    folded = partial_value.reshape(row_blocks, 1 << depth, -1, width)
    for which in range(depth):
        halves = folded.reshape(row_blocks, folded.shape[1] // 2, 2, folded.shape[2], width)
        mine = own_bit(which)
        keeping = lax.dynamic_index_in_dim(halves, mine, 2, keepdims=False)
        sending = lax.dynamic_index_in_dim(halves, 1 - mine, 2, keepdims=False)
        folded = keeping + partner(sending.astype(jnp.bfloat16), "row", which).astype(sending.dtype)
    return folded


def column_sum(partial_value, col_devs, mb):
    width = partial_value.shape[-1]
    shaped = partial_value.reshape(-1, col_devs, mb // col_devs, width)
    return lax.psum_scatter(shaped, "col", scatter_dimension=1, tiled=True)


def column_join(pieces):
    gathered = lax.all_gather(pieces, "col", axis=1, tiled=True)
    return gathered.reshape(-1, gathered.shape[-1])


def sibling_fold(values, which):
    mine = own_bit(which)
    keeping = lax.dynamic_index_in_dim(values, mine, 1, keepdims=True)
    sending = lax.dynamic_index_in_dim(values, 1 - mine, 1, keepdims=True)
    return keeping + partner(sending.astype(jnp.bfloat16), "row", which).astype(sending.dtype)


def parent_rows(values, which):
    other = partner(values, "row", which)
    first = jnp.concatenate((values, other), axis=1)
    second = jnp.concatenate((other, values), axis=1)
    joined = jnp.where(own_bit(which) == 0, first, second)
    return joined.reshape(joined.shape[0] * 2, 1, joined.shape[2], joined.shape[3])


def coupling(values, listings, depth, mb):
    row_count = values.shape[0]
    row_blocks = row_count // mb
    group = 1 << depth
    position = lax.axis_index("row")
    member = position // group
    local = position % group
    owned = jnp.arange(row_blocks, dtype=jnp.int32) * group + local
    listing = lax.dynamic_index_in_dim(listings, member, 0, keepdims=False)
    listed = jnp.any(listing[None, :, :] == owned[:, None, None], axis=-1)
    unit_width = values.shape[1] // listed.shape[1]
    keeping = jnp.repeat(jnp.repeat(listed, mb, axis=0), unit_width, axis=1)
    return jnp.where(keeping, values, jnp.zeros_like(values))


def per_device(dinv0, dinv1, dinv2, offdiag0, offdiag1, rhs0, rhs1, rhs2, block_rows0, block_rows1):
    col_devs = lax.axis_size("col")
    mb = dinv0.shape[1] * col_devs // block_rows0.shape[1]
    col_width = mb // col_devs
    width = rhs0.shape[1]
    lowest_group = lax.axis_size("row") // block_rows0.shape[0]
    groups = (lowest_group, 2 * lowest_group, 4 * lowest_group)
    if col_devs == 2 and col_width % 32 == 0:
        args = (
            dinv0, dinv1, dinv2, offdiag0, offdiag1, rhs0, rhs1, rhs2, block_rows0, block_rows1
        )
        return fused(args, groups, col_width)
    depths = tuple(group.bit_length() - 1 for group in groups)
    inverses = (dinv0, dinv1, dinv2)
    couplings = (
        coupling(offdiag0, block_rows0, depths[0], mb),
        coupling(offdiag1, block_rows1, depths[1], mb),
    )
    sides = (rhs0, rhs1, rhs2)

    def as_pieces(values):
        return values.reshape(-1, 1, col_width, width)

    solved = []
    residual = as_pieces(rhs0)
    for level in range(3):
        column_form = row_join(residual, depths[level])
        product = jnp.dot(inverses[level], column_form, preferred_element_type=jnp.float32)
        solved_pieces = column_sum(product, col_devs, mb).astype(jnp.bfloat16)
        solved.append(solved_pieces)
        if level < 2:
            solved_columns = row_join(solved_pieces, depths[level])
            partial_value = jnp.dot(
                couplings[level], solved_columns, preferred_element_type=jnp.float32
            )
            summed = column_sum(partial_value, col_devs, mb)
            summed = summed.reshape(summed.shape[0] // 2, 2, col_width, width)
            update = sibling_fold(summed, depths[level])
            residual = (as_pieces(sides[level + 1]).astype(jnp.float32) - update).astype(
                jnp.bfloat16
            )
    outputs = [None, None, None]
    weighted = solved[2]
    for level in (2, 1, 0):
        row_form = column_join(weighted)
        product = jnp.einsum(
            "ij,in->jn", inverses[level], row_form, preferred_element_type=jnp.float32
        )
        answer = row_fold(product, row_form.shape[0] // mb, depths[level])
        outputs[level] = answer.reshape(-1, width)
        if level > 0:
            child_pieces = parent_rows(answer.astype(jnp.bfloat16), depths[level - 1])
            child_form = column_join(child_pieces)
            partial_value = jnp.einsum(
                "ij,in->jn", couplings[level - 1], child_form, preferred_element_type=jnp.float32
            )
            carried = row_fold(partial_value, child_form.shape[0] // mb, depths[level - 1])
            weighted = (solved[level - 1].astype(jnp.float32) - carried).astype(jnp.bfloat16)
    return (outputs[0], outputs[1], outputs[2])


def solution(mesh):
    placed = (
        P("row", "col"),
        P("row", "col"),
        P("row", "col"),
        P("row", "col"),
        P("row", "col"),
        P(("row", "col"), None),
        P(("row", "col"), None),
        P(("row", "col"), None),
        P(),
        P(),
    )
    return jax.shard_map(
        per_device,
        mesh=mesh,
        in_specs=placed,
        out_specs=(P(("row", "col"), None), P(("row", "col"), None), P(("row", "col"), None)),
        check_vma=False,
    )
```

```python
import functools

import jax
import jax.numpy as jnp
from jax import lax
from jax.experimental import pallas as pl
from jax.experimental.pallas import tpu as pltpu
from jax.sharding import PartitionSpec as P

MESH = pl.DeviceIdType.MESH


class Exchange:
    def __init__(self, send_sems, recv_sems, row, col):
        self.send_sems, self.recv_sems = send_sems, recv_sems
        self.row, self.col = row, col
        self.used = 0
        self.sent = []

    def across(self, flips):
        where = self.row
        bit = 1
        while bit <= flips:
            if flips & bit:
                where = where + (1 - 2 * (self.row // bit % 2)) * bit
            bit *= 2
        return where

    def start(self, src, dst, flips=0, other_col=False):
        col = 1 - self.col if other_col else self.col
        copy = pltpu.make_async_remote_copy(
            src_ref=src,
            dst_ref=dst,
            send_sem=self.send_sems.at[self.used],
            recv_sem=self.recv_sems.at[self.used],
            device_id=(self.across(flips), col),
            device_id_type=MESH,
        )
        self.used += 1
        copy.start()
        self.sent.append(copy)
        return copy

    def finish(self):
        for copy in self.sent:
            copy.wait_send()


def solve_kernel(
    groups, blocks, n_cols, mc, width, others,
    dinv0, dinv1, dinv2, off0, off1, rhs0, rhs1, rhs2, list0, list1,
    out0, out1, out2,
    d0, d1, d2, l0, l1, b1, b2, n0, n1, mask,
    gr0, gr1, gr2, gx0, gx1,
    fp0, fp1, fp2, cp0, cp1,
    fr0, fr1, fr2, cr0, cr1,
    su0, su1, sb0, sb1, ub0, ub1,
    rw0, rw1, rw2, kw0, kw1, turned0, turned1, turned2,
    tf0, tf1, tf2, th0, th1, th2, kf0, kf1, kh0, kh1,
    tr0, tr1, tr2, kr0, kr1, zf, zh, zr, an0, an1, an2,
    send_sems, recv_sems, local_sems,
):
    row, col = lax.axis_index("row"), lax.axis_index("col")
    ex = Exchange(send_sems, recv_sems, row, col)
    mb = 2 * mc
    local = [row % g for g in groups]
    plane = groups[0]
    high = groups[2] // plane
    f32, bf16 = jnp.float32, jnp.bfloat16
    half_cols = n_cols // 2

    member0, member1 = row // groups[0], row // groups[1]
    pairs = [
        (rhs0, gr0.at[:, local[0]]), (dinv0, d0), (list0.at[member0], n0), (off0, l0),
        (list1.at[member1], n1), (dinv1, d1), (off1, l1), (dinv2, d2), (rhs1, b1), (rhs2, b2),
    ]
    loads = []
    for at, (src, dst) in enumerate(pairs):
        loads.append(pltpu.make_async_copy(src, dst, local_sems.at[at]))
        loads[-1].start()

    barrier = pltpu.get_barrier_semaphore()
    for flips in others:
        pl.semaphore_signal(barrier, inc=1, device_id=(ex.across(flips), col), device_id_type=MESH)
    pl.semaphore_signal(barrier, inc=1, device_id=(row, 1 - col), device_id_type=MESH)
    pl.semaphore_wait(barrier, len(others) + 1)

    def chunk(count, part):
        return pl.ds(part * (count // 2), count // 2)

    def gather(buf, level, part, src=None):
        at = chunk(blocks[level], part)
        mine = buf.at[at, local[level]]
        first = mine if src is None else src.at[at]
        return [ex.start(first, mine, k) for k in range(1, groups[level])]

    def gather_top_start(buf, part):
        mine = buf.at[chunk(blocks[2], part), local[2]]
        along = [ex.start(mine, mine, s * plane) for s in range(1, high)]
        return along, [ex.start(mine, mine, k) for k in range(1, plane)]

    def gather_top_on(buf, part, along, waits):
        for s in range(1, high):
            along[s - 1].wait_recv()
            slot = buf.at[chunk(blocks[2], part), ex.across(s * plane) % groups[2]]
            waits += [ex.start(slot, slot, k) for k in range(1, plane)]

    def received(copies):
        for copy in copies:
            copy.wait_recv()

    def apply_rows(matrix, buf, prod, level, out_part, in_part, add):
        count = blocks[level] // 2
        step = min(count, 256 // mb)
        cols = pl.ds(in_part * half_cols, half_cols)
        begin = out_part * count

        def body(i, carry):
            tile = matrix[pl.ds((begin + i * step) * mb, step * mb), cols]
            form = buf[chunk(blocks[level], in_part)].reshape(half_cols, width)
            res = jnp.dot(tile, form, preferred_element_type=f32)
            res = res.reshape(step, 2, mc, width)
            at = pl.ds(begin + i * step, step)
            prod[at] = prod[at] + res if add else res
            return carry

        lax.fori_loop(0, count // step, body, 0)

    def col_sum(prod, recv, level, part):
        at = chunk(blocks[level], part)
        return ex.start(prod.at[at, 1 - col], recv.at[at], other_col=True)

    def col_total(copy, prod, recv, level, part):
        copy.wait_recv()
        at = chunk(blocks[level], part)
        return prod[at, col] + recv[at]

    def build_mask(matrix, listing, level):
        count = blocks[level]
        owned = lax.broadcasted_iota(jnp.int32, (count, 1), 0) * groups[level] + local[level]
        listed = jnp.zeros((count, listing.shape[1]), f32)
        for k in range(listing.shape[0]):
            listed = listed + jnp.where(listing[k:k + 1, :] == owned, 1.0, 0.0)
        unit = lax.broadcasted_iota(jnp.int32, (listing.shape[1], n_cols), 1) // mc
        which = lax.broadcasted_iota(jnp.int32, (listing.shape[1], n_cols), 0)
        spread = jnp.where(unit == which, 1.0, 0.0).astype(bf16)
        mask[0:count, :] = jnp.dot(listed.astype(bf16), spread, preferred_element_type=f32)

        def body(i, carry):
            rows = pl.ds(i * mb, mb)
            keep = jnp.broadcast_to(mask[pl.ds(i, 1), :], (mb, n_cols)).astype(bf16)
            matrix[rows, :] = matrix[rows, :] * keep
            return carry

        lax.fori_loop(0, count, body, 0)

    def turn(form, turned, level, part):
        rows = blocks[level] // 2 * mb
        at = chunk(form.shape[0], part)
        turned[:, pl.ds(part * rows, rows)] = form[at].reshape(rows, width).T

    def apply_turned(matrix, turned, prod, half, level, out_part, in_part, add, last):
        count, group = blocks[level], groups[level]
        rows = pl.ds(in_part * (count // 2 * mb), count // 2 * mb)
        cols = max(256, mc * group)
        step = cols // (mc * group)
        tail = prod.shape[1:]

        def body(i, carry):
            begin = out_part * half_cols + i * cols
            tile = matrix[rows, pl.ds(pl.multiple_of(begin, cols), cols)]
            res = jnp.dot(turned[:, rows], tile, preferred_element_type=f32)
            res = res.T.reshape((step,) + tail)
            at = pl.ds(out_part * (count // 2) + i * step, step)
            if add:
                res = prod[at] + res
            prod[at] = res
            if last:
                half[at] = res.astype(bf16)
            return carry

        lax.fori_loop(0, half_cols // cols, body, 0)

    def fold(half, recv, level, part):
        group = groups[level]
        at = chunk(blocks[level], part)
        return [
            ex.start(half.at[at, ex.across(k) % group], recv.at[k - 1, at], k)
            for k in range(1, group)
        ]

    def folded(copies, prod, recv, level, part):
        at = chunk(blocks[level], part)
        total = prod[at, local[level]]
        for k, copy in enumerate(copies):
            copy.wait_recv()
            total = total + recv[k, at].astype(f32)
        return total

    def fold_top(half, recv, part):
        at = chunk(blocks[2], part)
        return [
            ex.start(half.at[at, :, ex.across(k) % plane], recv.at[k - 1, at], k)
            for k in range(1, plane)
        ]

    def fold_top_on(copies, prod, recv, part):
        at = chunk(blocks[2], part)
        total = prod[at, :, row % plane]
        for k, copy in enumerate(copies):
            copy.wait_recv()
            total = total + recv[k, at].astype(f32)
        zf[at] = total
        zh[at] = total.astype(bf16)
        return [
            ex.start(zh.at[at, ex.across(s * plane) // plane % high], zr.at[s - 1, at], s * plane)
            for s in range(1, high)
        ]

    def folded_top(copies, part):
        at = chunk(blocks[2], part)
        total = zf[at, row // plane % high]
        for s, copy in enumerate(copies):
            copy.wait_recv()
            total = total + zr[s, at].astype(f32)
        return total

    gathers = (gr0, gr1, gr2)
    solved = (gx0, gx1)
    inverses, couplings = (d0, d1, d2), (l0, l1)
    sides = (None, b1, b2)
    forms = (rw0, rw1, rw2)
    joins = [None, None]

    def start_join(level, part, weighted):
        at = chunk(blocks[level], part)
        forms[level][at, col] = weighted
        mine = forms[level].at[at, col]
        joins[part] = ex.start(mine, mine, other_col=True)

    arriving = [gather(gr0, 0, part, rhs0) for part in (0, 1)]
    for at in (2, 3):
        loads[at].wait()
    build_mask(l0, n0, 0)
    loads[1].wait()
    loads[0].wait()
    for level in range(3):
        matrix, buf = inverses[level], gathers[level]
        prod, recv = (fp0, fp1, fp2)[level], (fr0, fr1, fr2)[level]
        received(arriving[0])
        apply_rows(matrix, buf, prod, level, 0, 0, False)
        summing = col_sum(prod, recv, level, 0)
        apply_rows(matrix, buf, prod, level, 1, 0, False)
        spread = [None, None]
        for part in (0, 1):
            if part == 1:
                received(arriving[1])
                apply_rows(matrix, buf, prod, level, 1, 1, True)
                summing = col_sum(prod, recv, level, 1)
            found = col_total(summing, prod, recv, level, part).astype(bf16)
            if level == 2:
                start_join(2, part, found)
            else:
                solved[level][chunk(blocks[level], part), local[level]] = found
                spread[part] = gather(solved[level], level, part)
        if level == 2:
            break
        if level == 0:
            for at in (4, 5, 6, 7, 8, 9):
                loads[at].wait()
            build_mask(l1, n1, 1)
        matrix, buf = couplings[level], solved[level]
        prod, recv = (cp0, cp1)[level], (cr0, cr1)[level]
        received(spread[0])
        apply_rows(matrix, buf, prod, level, 0, 0, False)
        apply_rows(matrix, buf, prod, level, 1, 0, False)
        received(spread[1])
        summing = []
        for part in (0, 1):
            apply_rows(matrix, buf, prod, level, part, 1, True)
            summing.append(col_sum(prod, recv, level, part))
        keep, away, landed = (su0, su1)[level], (sb0, sb1)[level], (ub0, ub1)[level]
        side = row // groups[level] % 2
        moving = []
        for part in (0, 1):
            summed = col_total(summing[part], prod, recv, level, part)
            summed = summed.reshape(blocks[level] // 4, 2, mc, width)
            at = chunk(blocks[level + 1], part)
            keep[at] = summed
            away[at] = summed.astype(bf16)
            moving.append(ex.start(away.at[at, 1 - side], landed.at[at], groups[level]))
        arriving = [None, None]
        for part in (0, 1):
            moving[part].wait_recv()
            at = chunk(blocks[level + 1], part)
            update = keep[at, side] + landed[at].astype(f32)
            residual = (sides[level + 1][at].astype(f32) - update).astype(bf16)
            gathers[level + 1][at, local[level + 1]] = residual
            if level == 0:
                arriving[part] = gather(gr1, 1, part)
            else:
                arriving[part] = gather_top_start(gr2, part)
        if level == 1:
            for part in (0, 1):
                gather_top_on(gr2, part, *arriving[part])
            arriving = [waits for _, waits in arriving]

    stored = []
    for level in (2, 1, 0):
        matrix, form, turned = inverses[level], forms[level], (turned0, turned1, turned2)[level]
        prod, half = (tf0, tf1, tf2)[level], (th0, th1, th2)[level]
        recv = (tr0, tr1, tr2)[level]
        start = fold_top if level == 2 else functools.partial(fold, level=level)
        joins[1].wait_recv()
        turn(form, turned, level, 1)
        apply_turned(matrix, turned, prod, half, level, 1, 1, False, True)
        moving = [None, start(half, recv, part=1)]
        apply_turned(matrix, turned, prod, half, level, 0, 1, False, False)
        joins[0].wait_recv()
        turn(form, turned, level, 0)
        apply_turned(matrix, turned, prod, half, level, 0, 0, True, True)
        moving[0] = start(half, recv, part=0)
        if level == 2:
            for part in (1, 0):
                moving[part] = fold_top_on(moving[part], prod, recv, part)
        away, near = [None, None], [None, None]
        below = level - 1
        for part in (1, 0):
            at = chunk(blocks[level], part)
            if level == 2:
                answer = folded_top(moving[part], part)
            else:
                answer = folded(moving[part], prod, recv, level, part)
            if level > 0:
                side = row // groups[below] % 2
                child = (kw0, kw1)[below]
                child[at, side, col] = answer.astype(bf16)
                mine = child.at[at, side, col]
                away[part] = ex.start(mine, mine, groups[below])
                near[part] = ex.start(mine, mine, other_col=True)
            held, out = (an0, an1, an2)[level], (out0, out1, out2)[level]
            held[at] = answer
            stored.append(
                pltpu.make_async_copy(held.at[at], out.at[at], local_sems.at[10 + len(stored)])
            )
            stored[-1].start()
        if level == 0:
            break
        far = [None, None]
        for part in (1, 0):
            away[part].wait_recv()
            theirs = child.at[chunk(blocks[level], part), 1 - side, col]
            far[part] = ex.start(theirs, theirs, other_col=True)
        matrix, turned = couplings[below], (turned0, turned1)[below]
        prod, half, recv = (kf0, kf1)[below], (kh0, kh1)[below], (kr0, kr1)[below]
        near[1].wait_recv()
        far[1].wait_recv()
        turn(child, turned, below, 1)
        apply_turned(matrix, turned, prod, half, below, 1, 1, False, False)
        apply_turned(matrix, turned, prod, half, below, 0, 1, False, False)
        near[0].wait_recv()
        far[0].wait_recv()
        turn(child, turned, below, 0)
        moving = [None, None]
        for part in (1, 0):
            apply_turned(matrix, turned, prod, half, below, part, 0, True, True)
            moving[part] = fold(half, recv, below, part)
        for part in (1, 0):
            carried = folded(moving[part], prod, recv, below, part)
            own = solved[below][chunk(blocks[below], part), local[below]].astype(f32)
            start_join(below, part, (own - carried).astype(bf16))
    for copy in stored:
        copy.wait()
    ex.finish()


def hand_on(in0, in1, in2, out0, out1, out2, sems):
    copies = [
        pltpu.make_async_copy(src, dst, sems.at[at])
        for at, (src, dst) in enumerate(((in0, out0), (in1, out1), (in2, out2)))
    ]
    for copy in copies:
        copy.start()
    for copy in copies:
        copy.wait()


def fused(args, groups, mc):
    dinv0, dinv1, dinv2, off0, off1, rhs0, rhs1, rhs2, list0, list1 = args
    list0, list1 = jnp.swapaxes(list0, 1, 2), jnp.swapaxes(list1, 1, 2)
    n_cols = dinv0.shape[1]
    width = rhs0.shape[1]
    mb = 2 * mc
    blocks = [d.shape[0] // mb for d in (dinv0, dinv1, dinv2)]
    high = groups[2] // groups[0]
    others = sorted(set(range(1, groups[1])) | {s * groups[0] for s in range(1, high)} | {groups[1]})
    bf16, f32 = jnp.bfloat16, jnp.float32
    V = pltpu.VMEM
    r0, r1, r2 = blocks
    g0, g1, g2 = groups

    def unit(dtype, *lead):
        return V(lead + (mc, width), dtype)

    scratch = [V(a.shape, bf16) for a in (dinv0, dinv1, dinv2, off0, off1)]
    scratch += [unit(bf16, r1), unit(bf16, r2)]
    scratch += [V(a.shape[1:], jnp.int32) for a in (list0, list1)]
    scratch += [V((r0, n_cols), f32)]
    scratch += [unit(bf16, r, g) for r, g in ((r0, g0), (r1, g1), (r2, g2), (r0, g0), (r1, g1))]
    scratch += [unit(f32, r, 2) for r in (r0, r1, r2, r0, r1)]
    scratch += [unit(f32, r) for r in (r0, r1, r2, r0, r1)]
    scratch += [unit(f32, r0 // 2, 2), unit(f32, r1 // 2, 2)]
    scratch += [unit(bf16, r0 // 2, 2), unit(bf16, r1 // 2, 2)]
    scratch += [unit(bf16, r0 // 2), unit(bf16, r1 // 2)]
    scratch += [unit(bf16, r, 2) for r in (r0, r1, r2)]
    scratch += [unit(bf16, r0 // 2, 2, 2), unit(bf16, r1 // 2, 2, 2)]
    scratch += [V((width, r * mb), bf16) for r in blocks]
    top = (r2, high, g0)
    scratch += [unit(f32, r0, g0), unit(f32, r1, g1), unit(f32, *top)]
    scratch += [unit(bf16, r0, g0), unit(bf16, r1, g1), unit(bf16, *top)]
    scratch += [unit(f32, r0, g0), unit(f32, r1, g1)]
    scratch += [unit(bf16, r0, g0), unit(bf16, r1, g1)]
    scratch += [unit(bf16, g0 - 1, r0), unit(bf16, g1 - 1, r1), unit(bf16, g0 - 1, r2, high)]
    scratch += [unit(bf16, g0 - 1, r0), unit(bf16, g1 - 1, r1)]
    scratch += [unit(f32, r2, high), unit(bf16, r2, high), unit(bf16, high - 1, r2)]
    scratch += [unit(f32, r) for r in blocks]
    count = 2 * (4 * (g0 - 1) + 4 * (g1 - 1) + high * g0 + g0 + high + 16)
    scratch += [pltpu.SemaphoreType.DMA((count,)), pltpu.SemaphoreType.DMA((count,))]
    scratch += [pltpu.SemaphoreType.DMA((16,))]
    macs = sum(d.shape[0] for d in (dinv0, dinv1, dinv2, off0, off1)) * n_cols * width
    outs = pl.pallas_call(
        functools.partial(solve_kernel, groups, blocks, n_cols, mc, width, others),
        out_shape=[jax.ShapeDtypeStruct((r, mc, width), f32) for r in blocks],
        in_specs=[pl.BlockSpec(memory_space=pl.ANY)] * 10,
        out_specs=[pl.BlockSpec(memory_space=pl.ANY)] * 3,
        scratch_shapes=scratch,
        cost_estimate=pl.CostEstimate(
            flops=4 * macs, bytes_accessed=2 * macs // width, transcendentals=0
        ),
        compiler_params=pltpu.CompilerParams(
            collective_id=0, has_side_effects=True, vmem_limit_bytes=56 * 1024 * 1024
        ),
    )(
        dinv0, dinv1, dinv2, off0, off1,
        *[side.reshape(-1, mc, width) for side in (rhs0, rhs1, rhs2)],
        list0, list1,
    )
    outs = pl.pallas_call(
        hand_on,
        out_shape=[jax.ShapeDtypeStruct(out.shape, f32) for out in outs],
        in_specs=[pl.BlockSpec(memory_space=pl.ANY)] * 3,
        out_specs=[pl.BlockSpec(memory_space=pl.ANY)] * 3,
        scratch_shapes=[pltpu.SemaphoreType.DMA((3,))],
        cost_estimate=pl.CostEstimate(
            flops=0, bytes_accessed=8 * sum(blocks) * mc * width, transcendentals=0
        ),
        compiler_params=pltpu.CompilerParams(vmem_limit_bytes=56 * 1024 * 1024),
    )(*outs)
    return tuple(out.reshape(-1, width) for out in outs)


def partner(value, axis, stride):
    return lax.ppermute(value, axis, [(i, i ^ 1 << stride) for i in range(lax.axis_size(axis))])


def own_bit(which):
    return lax.axis_index("row") >> which & 1


def row_join(pieces, depth):
    joined = pieces
    for which in range(depth):
        other = partner(joined, "row", which)
        first = jnp.concatenate((joined, other), axis=1)
        second = jnp.concatenate((other, joined), axis=1)
        joined = jnp.where(own_bit(which) == 0, first, second)
    return joined.reshape(-1, joined.shape[-1])


def row_fold(partial_value, row_blocks, depth):
    width = partial_value.shape[-1]
    folded = partial_value.reshape(row_blocks, 1 << depth, -1, width)
    for which in range(depth):
        halves = folded.reshape(row_blocks, folded.shape[1] // 2, 2, folded.shape[2], width)
        mine = own_bit(which)
        keeping = lax.dynamic_index_in_dim(halves, mine, 2, keepdims=False)
        sending = lax.dynamic_index_in_dim(halves, 1 - mine, 2, keepdims=False)
        folded = keeping + partner(sending.astype(jnp.bfloat16), "row", which).astype(sending.dtype)
    return folded


def column_sum(partial_value, col_devs, mb):
    width = partial_value.shape[-1]
    shaped = partial_value.reshape(-1, col_devs, mb // col_devs, width)
    return lax.psum_scatter(shaped, "col", scatter_dimension=1, tiled=True)


def column_join(pieces):
    gathered = lax.all_gather(pieces, "col", axis=1, tiled=True)
    return gathered.reshape(-1, gathered.shape[-1])


def sibling_fold(values, which):
    mine = own_bit(which)
    keeping = lax.dynamic_index_in_dim(values, mine, 1, keepdims=True)
    sending = lax.dynamic_index_in_dim(values, 1 - mine, 1, keepdims=True)
    return keeping + partner(sending.astype(jnp.bfloat16), "row", which).astype(sending.dtype)


def parent_rows(values, which):
    other = partner(values, "row", which)
    first = jnp.concatenate((values, other), axis=1)
    second = jnp.concatenate((other, values), axis=1)
    joined = jnp.where(own_bit(which) == 0, first, second)
    return joined.reshape(joined.shape[0] * 2, 1, joined.shape[2], joined.shape[3])


def coupling(values, listings, depth, mb):
    row_count = values.shape[0]
    row_blocks = row_count // mb
    group = 1 << depth
    position = lax.axis_index("row")
    member = position // group
    local = position % group
    owned = jnp.arange(row_blocks, dtype=jnp.int32) * group + local
    listing = lax.dynamic_index_in_dim(listings, member, 0, keepdims=False)
    listed = jnp.any(listing[None, :, :] == owned[:, None, None], axis=-1)
    unit_width = values.shape[1] // listed.shape[1]
    keeping = jnp.repeat(jnp.repeat(listed, mb, axis=0), unit_width, axis=1)
    return jnp.where(keeping, values, jnp.zeros_like(values))


def per_device(dinv0, dinv1, dinv2, offdiag0, offdiag1, rhs0, rhs1, rhs2, block_rows0, block_rows1):
    col_devs = lax.axis_size("col")
    mb = dinv0.shape[1] * col_devs // block_rows0.shape[1]
    col_width = mb // col_devs
    width = rhs0.shape[1]
    lowest_group = lax.axis_size("row") // block_rows0.shape[0]
    groups = (lowest_group, 2 * lowest_group, 4 * lowest_group)
    if col_devs == 2 and col_width % 32 == 0:
        args = (
            dinv0, dinv1, dinv2, offdiag0, offdiag1, rhs0, rhs1, rhs2, block_rows0, block_rows1
        )
        return fused(args, groups, col_width)
    depths = tuple(group.bit_length() - 1 for group in groups)
    inverses = (dinv0, dinv1, dinv2)
    couplings = (
        coupling(offdiag0, block_rows0, depths[0], mb),
        coupling(offdiag1, block_rows1, depths[1], mb),
    )
    sides = (rhs0, rhs1, rhs2)

    def as_pieces(values):
        return values.reshape(-1, 1, col_width, width)

    solved = []
    residual = as_pieces(rhs0)
    for level in range(3):
        column_form = row_join(residual, depths[level])
        product = jnp.dot(inverses[level], column_form, preferred_element_type=jnp.float32)
        solved_pieces = column_sum(product, col_devs, mb).astype(jnp.bfloat16)
        solved.append(solved_pieces)
        if level < 2:
            solved_columns = row_join(solved_pieces, depths[level])
            partial_value = jnp.dot(
                couplings[level], solved_columns, preferred_element_type=jnp.float32
            )
            summed = column_sum(partial_value, col_devs, mb)
            summed = summed.reshape(summed.shape[0] // 2, 2, col_width, width)
            update = sibling_fold(summed, depths[level])
            residual = (as_pieces(sides[level + 1]).astype(jnp.float32) - update).astype(
                jnp.bfloat16
            )
    outputs = [None, None, None]
    weighted = solved[2]
    for level in (2, 1, 0):
        row_form = column_join(weighted)
        product = jnp.einsum(
            "ij,in->jn", inverses[level], row_form, preferred_element_type=jnp.float32
        )
        answer = row_fold(product, row_form.shape[0] // mb, depths[level])
        outputs[level] = answer.reshape(-1, width)
        if level > 0:
            child_pieces = parent_rows(answer.astype(jnp.bfloat16), depths[level - 1])
            child_form = column_join(child_pieces)
            partial_value = jnp.einsum(
                "ij,in->jn", couplings[level - 1], child_form, preferred_element_type=jnp.float32
            )
            carried = row_fold(partial_value, child_form.shape[0] // mb, depths[level - 1])
            weighted = (solved[level - 1].astype(jnp.float32) - carried).astype(jnp.bfloat16)
    return (outputs[0], outputs[1], outputs[2])


def solution(mesh):
    placed = (
        P("row", "col"),
        P("row", "col"),
        P("row", "col"),
        P("row", "col"),
        P("row", "col"),
        P(("row", "col"), None),
        P(("row", "col"), None),
        P(("row", "col"), None),
        P(),
        P(),
    )
    return jax.shard_map(
        per_device,
        mesh=mesh,
        in_specs=placed,
        out_specs=(P(("row", "col"), None), P(("row", "col"), None), P(("row", "col"), None)),
        check_vma=False,
    )
```

```python
import functools

import jax
import jax.numpy as jnp
from jax import lax
from jax.experimental import pallas as pl
from jax.experimental.pallas import tpu as pltpu
from jax.sharding import PartitionSpec as P

MESH = pl.DeviceIdType.MESH


class Exchange:
    def __init__(self, send_sems, recv_sems, row, col):
        self.send_sems, self.recv_sems = send_sems, recv_sems
        self.row, self.col = row, col
        self.used = 0
        self.sent = []

    def across(self, flips):
        where = self.row
        bit = 1
        while bit <= flips:
            if flips & bit:
                where = where + (1 - 2 * (self.row // bit % 2)) * bit
            bit *= 2
        return where

    def start(self, src, dst, flips=0, other_col=False):
        col = 1 - self.col if other_col else self.col
        copy = pltpu.make_async_remote_copy(
            src_ref=src,
            dst_ref=dst,
            send_sem=self.send_sems.at[self.used],
            recv_sem=self.recv_sems.at[self.used],
            device_id=(self.across(flips), col),
            device_id_type=MESH,
        )
        self.used += 1
        copy.start()
        self.sent.append(copy)
        return copy

    def finish(self):
        for copy in self.sent:
            copy.wait_send()


def solve_kernel(
    groups, blocks, n_cols, mc, width, others,
    dinv0, dinv1, dinv2, off0, off1, rhs0, rhs1, rhs2, list0, list1,
    out0, out1, out2,
    d0, d1, d2, l0, l1, b1, b2, n0, n1, mask,
    gr0, gr1, gr2, gx0, gx1,
    fp0, fp1, fp2, cp0, cp1,
    fr0, fr1, fr2, cr0, cr1,
    su0, su1, sb0, sb1, ub0, ub1,
    rw0, rw1, rw2, kw0, kw1, turned0, turned1, turned2,
    tf0, tf1, tf2, th0, th1, th2, kf0, kf1, kh0, kh1,
    tr0, tr1, tr2, kr0, kr1, zf, zh, zr, an0, an1, an2,
    send_sems, recv_sems, local_sems,
):
    row, col = lax.axis_index("row"), lax.axis_index("col")
    ex = Exchange(send_sems, recv_sems, row, col)
    mb = 2 * mc
    local = [row % g for g in groups]
    plane = groups[0]
    high = groups[2] // plane
    f32, bf16 = jnp.float32, jnp.bfloat16
    half_cols = n_cols // 2

    member0, member1 = row // groups[0], row // groups[1]
    pairs = [
        (rhs0, gr0.at[:, local[0]]), (dinv0, d0), (list0.at[member0], n0), (off0, l0),
        (list1.at[member1], n1), (dinv1, d1), (off1, l1), (dinv2, d2), (rhs1, b1), (rhs2, b2),
    ]
    loads = []
    for at, (src, dst) in enumerate(pairs):
        loads.append(pltpu.make_async_copy(src, dst, local_sems.at[at]))
        loads[-1].start()

    barrier = pltpu.get_barrier_semaphore()
    for flips in others:
        pl.semaphore_signal(barrier, inc=1, device_id=(ex.across(flips), col), device_id_type=MESH)
    pl.semaphore_signal(barrier, inc=1, device_id=(row, 1 - col), device_id_type=MESH)
    pl.semaphore_wait(barrier, len(others) + 1)

    def chunk(count, part):
        return pl.ds(part * (count // 2), count // 2)

    def gather(buf, level, part):
        at = chunk(blocks[level], part)
        mine = buf.at[at, local[level]]
        return [ex.start(mine, mine, k) for k in range(1, groups[level])]

    def gather_top_start(buf, part):
        mine = buf.at[chunk(blocks[2], part), local[2]]
        along = [ex.start(mine, mine, s * plane) for s in range(1, high)]
        return along, [ex.start(mine, mine, k) for k in range(1, plane)]

    def gather_top_on(buf, part, along, waits):
        for s in range(1, high):
            along[s - 1].wait_recv()
            slot = buf.at[chunk(blocks[2], part), ex.across(s * plane) % groups[2]]
            waits += [ex.start(slot, slot, k) for k in range(1, plane)]

    def received(copies):
        for copy in copies:
            copy.wait_recv()

    def apply_rows(matrix, buf, prod, level, out_part, in_part, add):
        count = blocks[level] // 2
        step = min(count, 256 // mb)
        cols = pl.ds(in_part * half_cols, half_cols)
        begin = out_part * count

        def body(i, carry):
            tile = matrix[pl.ds((begin + i * step) * mb, step * mb), cols]
            form = buf[chunk(blocks[level], in_part)].reshape(half_cols, width)
            res = jnp.dot(tile, form, preferred_element_type=f32)
            res = res.reshape(step, 2, mc, width)
            at = pl.ds(begin + i * step, step)
            prod[at] = prod[at] + res if add else res
            return carry

        lax.fori_loop(0, count // step, body, 0, unroll=True)

    def col_sum(prod, recv, level, part):
        at = chunk(blocks[level], part)
        return ex.start(prod.at[at, 1 - col], recv.at[at], other_col=True)

    def col_total(copy, prod, recv, level, part):
        copy.wait_recv()
        at = chunk(blocks[level], part)
        return prod[at, col] + recv[at]

    def build_mask(matrix, listing, level):
        count = blocks[level]
        owned = lax.broadcasted_iota(jnp.int32, (count, 1), 0) * groups[level] + local[level]
        listed = jnp.zeros((count, listing.shape[1]), f32)
        for k in range(listing.shape[0]):
            listed = listed + jnp.where(listing[k:k + 1, :] == owned, 1.0, 0.0)
        unit = lax.broadcasted_iota(jnp.int32, (listing.shape[1], n_cols), 1) // mc
        which = lax.broadcasted_iota(jnp.int32, (listing.shape[1], n_cols), 0)
        spread = jnp.where(unit == which, 1.0, 0.0).astype(bf16)
        mask[0:count, :] = jnp.dot(listed.astype(bf16), spread, preferred_element_type=f32)

        def body(i, carry):
            rows = pl.ds(i * mb, mb)
            keep = jnp.broadcast_to(mask[pl.ds(i, 1), :], (mb, n_cols)).astype(bf16)
            matrix[rows, :] = matrix[rows, :] * keep
            return carry

        lax.fori_loop(0, count, body, 0)

    def turn(form, turned, level, part):
        rows = blocks[level] // 2 * mb
        at = chunk(form.shape[0], part)
        turned[:, pl.ds(part * rows, rows)] = form[at].reshape(rows, width).T

    def apply_turned(matrix, turned, prod, half, level, out_part, whole):
        count, group = blocks[level], groups[level]
        rows = pl.ds(0, count * mb) if whole else pl.ds(count // 2 * mb, count // 2 * mb)
        cols = max(256, mc * group)
        step = cols // (mc * group)
        tail = prod.shape[1:]

        def body(i, carry):
            begin = out_part * half_cols + i * cols
            tile = matrix[rows, pl.ds(pl.multiple_of(begin, cols), cols)]
            res = jnp.dot(turned[:, rows], tile, preferred_element_type=f32)
            res = res.T.reshape((step,) + tail)
            at = pl.ds(out_part * (count // 2) + i * step, step)
            prod[at] = res
            half[at] = res.astype(bf16)
            return carry

        lax.fori_loop(0, half_cols // cols, body, 0, unroll=True)

    def fold(half, recv, level, part):
        group = groups[level]
        at = chunk(blocks[level], part)
        return [
            ex.start(half.at[at, ex.across(k) % group], recv.at[k - 1, at], k)
            for k in range(1, group)
        ]

    def folded(copies, prod, recv, level, part):
        at = chunk(blocks[level], part)
        total = prod[at, local[level]]
        for k, copy in enumerate(copies):
            copy.wait_recv()
            total = total + recv[k, at].astype(f32)
        return total

    def fold_top(half, recv, part):
        at = chunk(blocks[2], part)
        return [
            ex.start(half.at[at, :, ex.across(k) % plane], recv.at[k - 1, at], k)
            for k in range(1, plane)
        ]

    def fold_top_on(copies, prod, recv, part):
        at = chunk(blocks[2], part)
        total = prod[at, :, row % plane]
        for k, copy in enumerate(copies):
            copy.wait_recv()
            total = total + recv[k, at].astype(f32)
        zf[at] = total
        zh[at] = total.astype(bf16)
        return [
            ex.start(zh.at[at, ex.across(s * plane) // plane % high], zr.at[s - 1, at], s * plane)
            for s in range(1, high)
        ]

    def folded_top(copies, part):
        at = chunk(blocks[2], part)
        total = zf[at, row // plane % high]
        for s, copy in enumerate(copies):
            copy.wait_recv()
            total = total + zr[s, at].astype(f32)
        return total

    gathers = (gr0, gr1, gr2)
    solved = (gx0, gx1)
    inverses, couplings = (d0, d1, d2), (l0, l1)
    sides = (None, b1, b2)
    forms = (rw0, rw1, rw2)
    joins = [None, None]

    def start_join(level, part, weighted):
        at = chunk(blocks[level], part)
        forms[level][at, col] = weighted
        mine = forms[level].at[at, col]
        joins[part] = ex.start(mine, mine, other_col=True)

    loads[0].wait()
    arriving = [gather(gr0, 0, part) for part in (0, 1)]
    for at in (2, 3):
        loads[at].wait()
    build_mask(l0, n0, 0)
    loads[1].wait()
    for level in range(3):
        matrix, buf = inverses[level], gathers[level]
        prod, recv = (fp0, fp1, fp2)[level], (fr0, fr1, fr2)[level]
        received(arriving[0])
        apply_rows(matrix, buf, prod, level, 0, 0, False)
        summing = col_sum(prod, recv, level, 0)
        apply_rows(matrix, buf, prod, level, 1, 0, False)
        spread = [None, None]
        for part in (0, 1):
            if part == 1:
                received(arriving[1])
                apply_rows(matrix, buf, prod, level, 1, 1, True)
                summing = col_sum(prod, recv, level, 1)
            found = col_total(summing, prod, recv, level, part).astype(bf16)
            if level == 2:
                start_join(2, part, found)
            else:
                solved[level][chunk(blocks[level], part), local[level]] = found
                spread[part] = gather(solved[level], level, part)
        if level == 2:
            break
        if level == 0:
            for at in (4, 5, 6, 7, 8, 9):
                loads[at].wait()
            build_mask(l1, n1, 1)
        matrix, buf = couplings[level], solved[level]
        prod, recv = (cp0, cp1)[level], (cr0, cr1)[level]
        received(spread[0])
        apply_rows(matrix, buf, prod, level, 0, 0, False)
        apply_rows(matrix, buf, prod, level, 1, 0, False)
        received(spread[1])
        summing = []
        for part in (0, 1):
            apply_rows(matrix, buf, prod, level, part, 1, True)
            summing.append(col_sum(prod, recv, level, part))
        keep, away, landed = (su0, su1)[level], (sb0, sb1)[level], (ub0, ub1)[level]
        side = row // groups[level] % 2
        moving = []
        for part in (0, 1):
            summed = col_total(summing[part], prod, recv, level, part)
            summed = summed.reshape(blocks[level] // 4, 2, mc, width)
            at = chunk(blocks[level + 1], part)
            keep[at] = summed
            away[at] = summed.astype(bf16)
            moving.append(ex.start(away.at[at, 1 - side], landed.at[at], groups[level]))
        arriving = [None, None]
        for part in (0, 1):
            moving[part].wait_recv()
            at = chunk(blocks[level + 1], part)
            update = keep[at, side] + landed[at].astype(f32)
            residual = (sides[level + 1][at].astype(f32) - update).astype(bf16)
            gathers[level + 1][at, local[level + 1]] = residual
            if level == 0:
                arriving[part] = gather(gr1, 1, part)
            else:
                arriving[part] = gather_top_start(gr2, part)
        if level == 1:
            for part in (0, 1):
                gather_top_on(gr2, part, *arriving[part])
            arriving = [waits for _, waits in arriving]

    stored = []
    for level in (2, 1, 0):
        matrix, form, turned = inverses[level], forms[level], (turned0, turned1, turned2)[level]
        prod, half = (tf0, tf1, tf2)[level], (th0, th1, th2)[level]
        recv = (tr0, tr1, tr2)[level]
        start = fold_top if level == 2 else functools.partial(fold, level=level)
        joins[1].wait_recv()
        turn(form, turned, level, 1)
        apply_turned(matrix, turned, prod, half, level, 1, False)
        moving = [None, start(half, recv, part=1)]
        joins[0].wait_recv()
        turn(form, turned, level, 0)
        apply_turned(matrix, turned, prod, half, level, 0, True)
        moving[0] = start(half, recv, part=0)
        if level == 2:
            for part in (1, 0):
                moving[part] = fold_top_on(moving[part], prod, recv, part)
        away, near = [None, None], [None, None]
        below = level - 1
        for part in (1, 0):
            at = chunk(blocks[level], part)
            if level == 2:
                answer = folded_top(moving[part], part)
            else:
                answer = folded(moving[part], prod, recv, level, part)
            if level > 0:
                side = row // groups[below] % 2
                child = (kw0, kw1)[below]
                child[at, side, col] = answer.astype(bf16)
                mine = child.at[at, side, col]
                away[part] = ex.start(mine, mine, groups[below])
                near[part] = ex.start(mine, mine, other_col=True)
            held, out = (an0, an1, an2)[level], (out0, out1, out2)[level]
            held[at] = answer
            stored.append(
                pltpu.make_async_copy(held.at[at], out.at[at], local_sems.at[10 + len(stored)])
            )
            stored[-1].start()
        if level == 0:
            break
        far = [None, None]
        for part in (1, 0):
            away[part].wait_recv()
            theirs = child.at[chunk(blocks[level], part), 1 - side, col]
            far[part] = ex.start(theirs, theirs, other_col=True)
        matrix, turned = couplings[below], (turned0, turned1)[below]
        prod, half, recv = (kf0, kf1)[below], (kh0, kh1)[below], (kr0, kr1)[below]
        near[1].wait_recv()
        far[1].wait_recv()
        turn(child, turned, below, 1)
        near[0].wait_recv()
        far[0].wait_recv()
        turn(child, turned, below, 0)
        moving = [None, None]
        for part in (1, 0):
            apply_turned(matrix, turned, prod, half, below, part, True)
            moving[part] = fold(half, recv, below, part)
        for part in (1, 0):
            carried = folded(moving[part], prod, recv, below, part)
            own = solved[below][chunk(blocks[below], part), local[below]].astype(f32)
            start_join(below, part, (own - carried).astype(bf16))
    for copy in stored:
        copy.wait()
    ex.finish()


def hand_on(in0, in1, in2, out0, out1, out2, held0, held1, held2, sems):
    triples = ((in0, held0, out0), (in1, held1, out1), (in2, held2, out2))
    inward = [pltpu.make_async_copy(a, b, sems.at[at]) for at, (a, b, _) in enumerate(triples)]
    outward = [
        pltpu.make_async_copy(b, c, sems.at[3 + at]) for at, (_, b, c) in enumerate(triples)
    ]
    for copy in inward:
        copy.start()
    for first, second in zip(inward, outward):
        first.wait()
        second.start()
    for copy in outward:
        copy.wait()


def fused(args, groups, mc):
    dinv0, dinv1, dinv2, off0, off1, rhs0, rhs1, rhs2, list0, list1 = args
    list0, list1 = jnp.swapaxes(list0, 1, 2), jnp.swapaxes(list1, 1, 2)
    n_cols = dinv0.shape[1]
    width = rhs0.shape[1]
    mb = 2 * mc
    blocks = [d.shape[0] // mb for d in (dinv0, dinv1, dinv2)]
    high = groups[2] // groups[0]
    others = sorted(set(range(1, groups[1])) | {s * groups[0] for s in range(1, high)} | {groups[1]})
    bf16, f32 = jnp.bfloat16, jnp.float32
    V = pltpu.VMEM
    r0, r1, r2 = blocks
    g0, g1, g2 = groups

    def unit(dtype, *lead):
        return V(lead + (mc, width), dtype)

    scratch = [V(a.shape, bf16) for a in (dinv0, dinv1, dinv2, off0, off1)]
    scratch += [unit(bf16, r1), unit(bf16, r2)]
    scratch += [V(a.shape[1:], jnp.int32) for a in (list0, list1)]
    scratch += [V((r0, n_cols), f32)]
    scratch += [unit(bf16, r, g) for r, g in ((r0, g0), (r1, g1), (r2, g2), (r0, g0), (r1, g1))]
    scratch += [unit(f32, r, 2) for r in (r0, r1, r2, r0, r1)]
    scratch += [unit(f32, r) for r in (r0, r1, r2, r0, r1)]
    scratch += [unit(f32, r0 // 2, 2), unit(f32, r1 // 2, 2)]
    scratch += [unit(bf16, r0 // 2, 2), unit(bf16, r1 // 2, 2)]
    scratch += [unit(bf16, r0 // 2), unit(bf16, r1 // 2)]
    scratch += [unit(bf16, r, 2) for r in (r0, r1, r2)]
    scratch += [unit(bf16, r0 // 2, 2, 2), unit(bf16, r1 // 2, 2, 2)]
    scratch += [V((width, r * mb), bf16) for r in blocks]
    top = (r2, high, g0)
    scratch += [unit(f32, r0, g0), unit(f32, r1, g1), unit(f32, *top)]
    scratch += [unit(bf16, r0, g0), unit(bf16, r1, g1), unit(bf16, *top)]
    scratch += [unit(f32, r0, g0), unit(f32, r1, g1)]
    scratch += [unit(bf16, r0, g0), unit(bf16, r1, g1)]
    scratch += [unit(bf16, g0 - 1, r0), unit(bf16, g1 - 1, r1), unit(bf16, g0 - 1, r2, high)]
    scratch += [unit(bf16, g0 - 1, r0), unit(bf16, g1 - 1, r1)]
    scratch += [unit(f32, r2, high), unit(bf16, r2, high), unit(bf16, high - 1, r2)]
    scratch += [unit(f32, r) for r in blocks]
    count = 2 * (4 * (g0 - 1) + 4 * (g1 - 1) + high * g0 + g0 + high + 16)
    scratch += [pltpu.SemaphoreType.DMA((count,)), pltpu.SemaphoreType.DMA((count,))]
    scratch += [pltpu.SemaphoreType.DMA((16,))]
    macs = sum(d.shape[0] for d in (dinv0, dinv1, dinv2, off0, off1)) * n_cols * width
    outs = pl.pallas_call(
        functools.partial(solve_kernel, groups, blocks, n_cols, mc, width, others),
        out_shape=[jax.ShapeDtypeStruct((r, mc, width), f32) for r in blocks],
        in_specs=[pl.BlockSpec(memory_space=pl.ANY)] * 10,
        out_specs=[pl.BlockSpec(memory_space=pl.ANY)] * 3,
        scratch_shapes=scratch,
        cost_estimate=pl.CostEstimate(
            flops=4 * macs, bytes_accessed=2 * macs // width, transcendentals=0
        ),
        compiler_params=pltpu.CompilerParams(
            collective_id=0, has_side_effects=True, vmem_limit_bytes=56 * 1024 * 1024
        ),
    )(
        dinv0, dinv1, dinv2, off0, off1,
        *[side.reshape(-1, mc, width) for side in (rhs0, rhs1, rhs2)],
        list0, list1,
    )
    outs = pl.pallas_call(
        hand_on,
        out_shape=[jax.ShapeDtypeStruct(out.shape, f32) for out in outs],
        in_specs=[pl.BlockSpec(memory_space=pl.ANY)] * 3,
        out_specs=[pl.BlockSpec(memory_space=pl.ANY)] * 3,
        scratch_shapes=[unit(f32, r) for r in blocks] + [pltpu.SemaphoreType.DMA((6,))],
        cost_estimate=pl.CostEstimate(
            flops=0, bytes_accessed=8 * sum(blocks) * mc * width, transcendentals=0
        ),
        compiler_params=pltpu.CompilerParams(vmem_limit_bytes=56 * 1024 * 1024),
    )(*outs)
    return tuple(out.reshape(-1, width) for out in outs)


def partner(value, axis, stride):
    return lax.ppermute(value, axis, [(i, i ^ 1 << stride) for i in range(lax.axis_size(axis))])


def own_bit(which):
    return lax.axis_index("row") >> which & 1


def row_join(pieces, depth):
    joined = pieces
    for which in range(depth):
        other = partner(joined, "row", which)
        first = jnp.concatenate((joined, other), axis=1)
        second = jnp.concatenate((other, joined), axis=1)
        joined = jnp.where(own_bit(which) == 0, first, second)
    return joined.reshape(-1, joined.shape[-1])


def row_fold(partial_value, row_blocks, depth):
    width = partial_value.shape[-1]
    folded = partial_value.reshape(row_blocks, 1 << depth, -1, width)
    for which in range(depth):
        halves = folded.reshape(row_blocks, folded.shape[1] // 2, 2, folded.shape[2], width)
        mine = own_bit(which)
        keeping = lax.dynamic_index_in_dim(halves, mine, 2, keepdims=False)
        sending = lax.dynamic_index_in_dim(halves, 1 - mine, 2, keepdims=False)
        folded = keeping + partner(sending.astype(jnp.bfloat16), "row", which).astype(sending.dtype)
    return folded


def column_sum(partial_value, col_devs, mb):
    width = partial_value.shape[-1]
    shaped = partial_value.reshape(-1, col_devs, mb // col_devs, width)
    return lax.psum_scatter(shaped, "col", scatter_dimension=1, tiled=True)


def column_join(pieces):
    gathered = lax.all_gather(pieces, "col", axis=1, tiled=True)
    return gathered.reshape(-1, gathered.shape[-1])


def sibling_fold(values, which):
    mine = own_bit(which)
    keeping = lax.dynamic_index_in_dim(values, mine, 1, keepdims=True)
    sending = lax.dynamic_index_in_dim(values, 1 - mine, 1, keepdims=True)
    return keeping + partner(sending.astype(jnp.bfloat16), "row", which).astype(sending.dtype)


def parent_rows(values, which):
    other = partner(values, "row", which)
    first = jnp.concatenate((values, other), axis=1)
    second = jnp.concatenate((other, values), axis=1)
    joined = jnp.where(own_bit(which) == 0, first, second)
    return joined.reshape(joined.shape[0] * 2, 1, joined.shape[2], joined.shape[3])


def coupling(values, listings, depth, mb):
    row_count = values.shape[0]
    row_blocks = row_count // mb
    group = 1 << depth
    position = lax.axis_index("row")
    member = position // group
    local = position % group
    owned = jnp.arange(row_blocks, dtype=jnp.int32) * group + local
    listing = lax.dynamic_index_in_dim(listings, member, 0, keepdims=False)
    listed = jnp.any(listing[None, :, :] == owned[:, None, None], axis=-1)
    unit_width = values.shape[1] // listed.shape[1]
    keeping = jnp.repeat(jnp.repeat(listed, mb, axis=0), unit_width, axis=1)
    return jnp.where(keeping, values, jnp.zeros_like(values))


def per_device(dinv0, dinv1, dinv2, offdiag0, offdiag1, rhs0, rhs1, rhs2, block_rows0, block_rows1):
    col_devs = lax.axis_size("col")
    mb = dinv0.shape[1] * col_devs // block_rows0.shape[1]
    col_width = mb // col_devs
    width = rhs0.shape[1]
    lowest_group = lax.axis_size("row") // block_rows0.shape[0]
    groups = (lowest_group, 2 * lowest_group, 4 * lowest_group)
    if col_devs == 2 and col_width % 32 == 0:
        args = (
            dinv0, dinv1, dinv2, offdiag0, offdiag1, rhs0, rhs1, rhs2, block_rows0, block_rows1
        )
        return fused(args, groups, col_width)
    depths = tuple(group.bit_length() - 1 for group in groups)
    inverses = (dinv0, dinv1, dinv2)
    couplings = (
        coupling(offdiag0, block_rows0, depths[0], mb),
        coupling(offdiag1, block_rows1, depths[1], mb),
    )
    sides = (rhs0, rhs1, rhs2)

    def as_pieces(values):
        return values.reshape(-1, 1, col_width, width)

    solved = []
    residual = as_pieces(rhs0)
    for level in range(3):
        column_form = row_join(residual, depths[level])
        product = jnp.dot(inverses[level], column_form, preferred_element_type=jnp.float32)
        solved_pieces = column_sum(product, col_devs, mb).astype(jnp.bfloat16)
        solved.append(solved_pieces)
        if level < 2:
            solved_columns = row_join(solved_pieces, depths[level])
            partial_value = jnp.dot(
                couplings[level], solved_columns, preferred_element_type=jnp.float32
            )
            summed = column_sum(partial_value, col_devs, mb)
            summed = summed.reshape(summed.shape[0] // 2, 2, col_width, width)
            update = sibling_fold(summed, depths[level])
            residual = (as_pieces(sides[level + 1]).astype(jnp.float32) - update).astype(
                jnp.bfloat16
            )
    outputs = [None, None, None]
    weighted = solved[2]
    for level in (2, 1, 0):
        row_form = column_join(weighted)
        product = jnp.einsum(
            "ij,in->jn", inverses[level], row_form, preferred_element_type=jnp.float32
        )
        answer = row_fold(product, row_form.shape[0] // mb, depths[level])
        outputs[level] = answer.reshape(-1, width)
        if level > 0:
            child_pieces = parent_rows(answer.astype(jnp.bfloat16), depths[level - 1])
            child_form = column_join(child_pieces)
            partial_value = jnp.einsum(
                "ij,in->jn", couplings[level - 1], child_form, preferred_element_type=jnp.float32
            )
            carried = row_fold(partial_value, child_form.shape[0] // mb, depths[level - 1])
            weighted = (solved[level - 1].astype(jnp.float32) - carried).astype(jnp.bfloat16)
    return (outputs[0], outputs[1], outputs[2])


def solution(mesh):
    placed = (
        P("row", "col"),
        P("row", "col"),
        P("row", "col"),
        P("row", "col"),
        P("row", "col"),
        P(("row", "col"), None),
        P(("row", "col"), None),
        P(("row", "col"), None),
        P(),
        P(),
    )
    return jax.shard_map(
        per_device,
        mesh=mesh,
        in_specs=placed,
        out_specs=(P(("row", "col"), None), P(("row", "col"), None), P(("row", "col"), None)),
        check_vma=False,
    )
```

```python
import functools

import jax
import jax.numpy as jnp
from jax import lax
from jax.experimental import pallas as pl
from jax.experimental.pallas import tpu as pltpu
from jax.sharding import PartitionSpec as P

MESH = pl.DeviceIdType.MESH


class Exchange:
    def __init__(self, send_sems, recv_sems, row, col):
        self.send_sems, self.recv_sems = send_sems, recv_sems
        self.row, self.col = row, col
        self.used = 0
        self.sent = []

    def across(self, flips):
        where = self.row
        bit = 1
        while bit <= flips:
            if flips & bit:
                where = where + (1 - 2 * (self.row // bit % 2)) * bit
            bit *= 2
        return where

    def start(self, src, dst, flips=0, other_col=False):
        col = 1 - self.col if other_col else self.col
        copy = pltpu.make_async_remote_copy(
            src_ref=src,
            dst_ref=dst,
            send_sem=self.send_sems.at[self.used],
            recv_sem=self.recv_sems.at[self.used],
            device_id=(self.across(flips), col),
            device_id_type=MESH,
        )
        self.used += 1
        copy.start()
        self.sent.append(copy)
        return copy

    def finish(self):
        for copy in self.sent:
            copy.wait_send()


def solve_kernel(
    groups, blocks, parts, n_cols, mc, width, others,
    dinv0, dinv1, dinv2, off0, off1, rhs0, rhs1, rhs2, list0, list1,
    out0, out1, out2,
    d0, d1, d2, l0, l1, b1, b2, n0, n1, mask,
    gr0, gr1, gr2, gx0, gx1,
    fp0, fp1, fp2, cp0, cp1,
    fr0, fr1, fr2, cr0, cr1,
    su0, su1, sb0, sb1, ub0, ub1,
    rw0, rw1, rw2, kw0, kw1, turned0, turned1, turned2,
    tf0, tf1, tf2, th0, th1, th2, kf0, kf1, kh0, kh1,
    tr0, tr1, tr2, kr0, kr1, zf, zh, zr, an0, an1, an2,
    send_sems, recv_sems, local_sems,
):
    row, col = lax.axis_index("row"), lax.axis_index("col")
    ex = Exchange(send_sems, recv_sems, row, col)
    mb = 2 * mc
    local = [row % g for g in groups]
    plane = groups[0]
    high = groups[2] // plane
    f32, bf16 = jnp.float32, jnp.bfloat16

    member0, member1 = row // groups[0], row // groups[1]
    pairs = [
        (rhs0, gr0.at[:, local[0]]), (dinv0, d0), (list0.at[member0], n0), (off0, l0),
        (list1.at[member1], n1), (dinv1, d1), (off1, l1), (dinv2, d2), (rhs1, b1), (rhs2, b2),
    ]
    loads = []
    for at, (src, dst) in enumerate(pairs):
        loads.append(pltpu.make_async_copy(src, dst, local_sems.at[at]))
        loads[-1].start()

    barrier = pltpu.get_barrier_semaphore()
    for flips in others:
        pl.semaphore_signal(barrier, inc=1, device_id=(ex.across(flips), col), device_id_type=MESH)
    pl.semaphore_signal(barrier, inc=1, device_id=(row, 1 - col), device_id_type=MESH)
    pl.semaphore_wait(barrier, len(others) + 1)

    def chunk(count, part, total):
        return pl.ds(part * (count // total), count // total)

    def span(level, part):
        return chunk(blocks[level], part, parts[level])

    def gather(buf, level, part):
        at = span(level, part)
        mine = buf.at[at, local[level]]
        return [ex.start(mine, mine, k) for k in range(1, groups[level])]

    def gather_top_start(buf, part):
        mine = buf.at[span(2, part), local[2]]
        along = [ex.start(mine, mine, s * plane) for s in range(1, high)]
        return along, [ex.start(mine, mine, k) for k in range(1, plane)]

    def gather_top_on(buf, part, along, waits):
        for s in range(1, high):
            along[s - 1].wait_recv()
            slot = buf.at[span(2, part), ex.across(s * plane) % groups[2]]
            waits += [ex.start(slot, slot, k) for k in range(1, plane)]

    def received(copies):
        for copy in copies:
            copy.wait_recv()

    def apply_rows(matrix, buf, prod, level, begin, count, in_part, add):
        step = min(count, 256 // mb)
        width_in = n_cols // parts[level]
        cols = pl.ds(in_part * width_in, width_in)

        def body(i, carry):
            tile = matrix[pl.ds((begin + i * step) * mb, step * mb), cols]
            form = buf[span(level, in_part)].reshape(width_in, width)
            res = jnp.dot(tile, form, preferred_element_type=f32)
            res = res.reshape(step, 2, mc, width)
            at = pl.ds(begin + i * step, step)
            prod[at] = prod[at] + res if add else res
            return carry

        lax.fori_loop(0, count // step, body, 0, unroll=True)

    def col_sum(prod, recv, at):
        return ex.start(prod.at[at, 1 - col], recv.at[at], other_col=True)

    def col_total(copy, prod, recv, at):
        copy.wait_recv()
        return prod[at, col] + recv[at]

    def build_mask(matrix, listing, level):
        count = blocks[level]
        owned = lax.broadcasted_iota(jnp.int32, (count, 1), 0) * groups[level] + local[level]
        listed = jnp.zeros((count, listing.shape[1]), f32)
        for k in range(listing.shape[0]):
            listed = listed + jnp.where(listing[k:k + 1, :] == owned, 1.0, 0.0)
        unit = lax.broadcasted_iota(jnp.int32, (listing.shape[1], n_cols), 1) // mc
        which = lax.broadcasted_iota(jnp.int32, (listing.shape[1], n_cols), 0)
        spread = jnp.where(unit == which, 1.0, 0.0).astype(bf16)
        mask[0:count, :] = jnp.dot(listed.astype(bf16), spread, preferred_element_type=f32)

        def body(i, carry):
            rows = pl.ds(i * mb, mb)
            keep = jnp.broadcast_to(mask[pl.ds(i, 1), :], (mb, n_cols)).astype(bf16)
            matrix[rows, :] = matrix[rows, :] * keep
            return carry

        lax.fori_loop(0, count, body, 0)

    def turn(form, turned, part, total):
        rows = turned.shape[1] // total
        at = chunk(form.shape[0], part, total)
        turned[:, pl.ds(part * rows, rows)] = form[at].reshape(rows, width).T

    def apply_turned(matrix, turned, prod, half, level, out_part, in_part):
        count, group = blocks[level], groups[level]
        skip = in_part * (count // parts[level] * mb)
        rows = pl.ds(skip, count * mb - skip)
        cols = max(256, mc * group)
        step = cols // (mc * group)
        tail = prod.shape[1:]

        def body(i, carry):
            begin = out_part * (n_cols // parts[level]) + i * cols
            tile = matrix[rows, pl.ds(pl.multiple_of(begin, cols), cols)]
            res = jnp.dot(turned[:, rows], tile, preferred_element_type=f32)
            res = res.T.reshape((step,) + tail)
            at = pl.ds(out_part * (count // parts[level]) + i * step, step)
            prod[at] = res
            half[at] = res.astype(bf16)
            return carry

        lax.fori_loop(0, n_cols // parts[level] // cols, body, 0, unroll=True)

    def fold(half, recv, level, part):
        group = groups[level]
        at = span(level, part)
        return [
            ex.start(half.at[at, ex.across(k) % group], recv.at[k - 1, at], k)
            for k in range(1, group)
        ]

    def folded(copies, prod, recv, level, part):
        at = span(level, part)
        total = prod[at, local[level]]
        for k, copy in enumerate(copies):
            copy.wait_recv()
            total = total + recv[k, at].astype(f32)
        return total

    def fold_top(half, recv, part):
        at = span(2, part)
        return [
            ex.start(half.at[at, :, ex.across(k) % plane], recv.at[k - 1, at], k)
            for k in range(1, plane)
        ]

    def fold_top_on(copies, prod, recv, part):
        at = span(2, part)
        total = prod[at, :, row % plane]
        for k, copy in enumerate(copies):
            copy.wait_recv()
            total = total + recv[k, at].astype(f32)
        zf[at] = total
        zh[at] = total.astype(bf16)
        return [
            ex.start(zh.at[at, ex.across(s * plane) // plane % high], zr.at[s - 1, at], s * plane)
            for s in range(1, high)
        ]

    def folded_top(copies, part):
        at = span(2, part)
        total = zf[at, row // plane % high]
        for s, copy in enumerate(copies):
            copy.wait_recv()
            total = total + zr[s, at].astype(f32)
        return total

    gathers = (gr0, gr1, gr2)
    solved = (gx0, gx1)
    inverses, couplings = (d0, d1, d2), (l0, l1)
    sides = (None, b1, b2)
    forms = (rw0, rw1, rw2)
    joins = {}

    def start_join(level, part, weighted):
        at = span(level, part)
        forms[level][at, col] = weighted
        mine = forms[level].at[at, col]
        joins[part] = ex.start(mine, mine, other_col=True)

    loads[0].wait()
    arriving = [gather(gr0, 0, part) for part in range(parts[0])]
    loads[1].wait()
    for level in range(3):
        matrix, buf = inverses[level], gathers[level]
        prod, recv = (fp0, fp1, fp2)[level], (fr0, fr1, fr2)[level]
        size = blocks[level] // parts[level]
        spread = []
        for part in range(parts[level]):
            at, after = span(level, part), (part + 1) * size
            received(arriving[part])
            apply_rows(matrix, buf, prod, level, part * size, size, part, part > 0)
            summing = col_sum(prod, recv, at)
            if after < blocks[level]:
                apply_rows(matrix, buf, prod, level, after, blocks[level] - after, part, part > 0)
            found = col_total(summing, prod, recv, at).astype(bf16)
            if level == 2:
                start_join(2, part, found)
            else:
                solved[level][at, local[level]] = found
                spread.append(gather(solved[level], level, part))
        if level == 2:
            break
        if level == 0:
            for at in range(2, 10):
                loads[at].wait()
        build_mask(couplings[level], (n0, n1)[level], level)
        matrix, buf = couplings[level], solved[level]
        prod, recv = (cp0, cp1)[level], (cr0, cr1)[level]
        last = parts[level] - 1
        for part in range(last):
            received(spread[part])
            apply_rows(matrix, buf, prod, level, 0, blocks[level], part, part > 0)
        received(spread[last])
        steps = range(parts[level + 1])
        size = blocks[level] // len(steps)
        summing = []
        for part in steps:
            apply_rows(matrix, buf, prod, level, part * size, size, last, last > 0)
            summing.append(col_sum(prod, recv, chunk(blocks[level], part, len(steps))))
        keep, away, landed = (su0, su1)[level], (sb0, sb1)[level], (ub0, ub1)[level]
        side = row // groups[level] % 2
        moving = []
        for part in steps:
            summed = col_total(
                summing[part], prod, recv, chunk(blocks[level], part, len(steps))
            )
            summed = summed.reshape(size // 2, 2, mc, width)
            at = span(level + 1, part)
            keep[at] = summed
            away[at] = summed.astype(bf16)
            moving.append(ex.start(away.at[at, 1 - side], landed.at[at], groups[level]))
        arriving = []
        for part in steps:
            moving[part].wait_recv()
            at = span(level + 1, part)
            update = keep[at, side] + landed[at].astype(f32)
            residual = (sides[level + 1][at].astype(f32) - update).astype(bf16)
            gathers[level + 1][at, local[level + 1]] = residual
            if level == 0:
                arriving.append(gather(gr1, 1, part))
            else:
                arriving.append(gather_top_start(gr2, part))
        if level == 1:
            for part in steps:
                gather_top_on(gr2, part, *arriving[part])
            arriving = [waits for _, waits in arriving]

    stored = []
    for level in (2, 1, 0):
        matrix, form, turned = inverses[level], forms[level], (turned0, turned1, turned2)[level]
        prod, half = (tf0, tf1, tf2)[level], (th0, th1, th2)[level]
        recv = (tr0, tr1, tr2)[level]
        start = fold_top if level == 2 else functools.partial(fold, level=level)
        steps = range(parts[level] - 1, -1, -1)
        moving = {}
        for part in steps:
            joins[part].wait_recv()
            turn(form, turned, part, len(steps))
            apply_turned(matrix, turned, prod, half, level, part, part)
            moving[part] = start(half, recv, part=part)
        if level == 2:
            for part in steps:
                moving[part] = fold_top_on(moving[part], prod, recv, part)
        away, near, far = {}, {}, {}
        below = level - 1
        for part in steps:
            at = span(level, part)
            if level == 2:
                answer = folded_top(moving[part], part)
            else:
                answer = folded(moving[part], prod, recv, level, part)
            if level > 0:
                side = row // groups[below] % 2
                child = (kw0, kw1)[below]
                child[at, side, col] = answer.astype(bf16)
                mine = child.at[at, side, col]
                away[part] = ex.start(mine, mine, groups[below])
                near[part] = ex.start(mine, mine, other_col=True)
            held, out = (an0, an1, an2)[level], (out0, out1, out2)[level]
            held[at] = answer
            stored.append(
                pltpu.make_async_copy(held.at[at], out.at[at], local_sems.at[10 + len(stored)])
            )
            stored[-1].start()
        if level == 0:
            break
        for part in steps:
            away[part].wait_recv()
            theirs = child.at[span(level, part), 1 - side, col]
            far[part] = ex.start(theirs, theirs, other_col=True)
        matrix, turned = couplings[below], (turned0, turned1)[below]
        prod, half, recv = (kf0, kf1)[below], (kh0, kh1)[below], (kr0, kr1)[below]
        for part in steps:
            near[part].wait_recv()
            far[part].wait_recv()
            turn(child, turned, part, len(steps))
        moving = {}
        for part in range(parts[below] - 1, -1, -1):
            apply_turned(matrix, turned, prod, half, below, part, 0)
            moving[part] = fold(half, recv, below, part)
        for part in range(parts[below] - 1, -1, -1):
            carried = folded(moving[part], prod, recv, below, part)
            own = solved[below][span(below, part), local[below]].astype(f32)
            start_join(below, part, (own - carried).astype(bf16))
    for copy in stored:
        copy.wait()
    ex.finish()


def hand_on(in0, in1, in2, out0, out1, out2, held0, held1, held2, sems):
    triples = ((in0, held0, out0), (in1, held1, out1), (in2, held2, out2))
    inward = [pltpu.make_async_copy(a, b, sems.at[at]) for at, (a, b, _) in enumerate(triples)]
    outward = [
        pltpu.make_async_copy(b, c, sems.at[3 + at]) for at, (_, b, c) in enumerate(triples)
    ]
    for copy in inward:
        copy.start()
    for first, second in zip(inward, outward):
        first.wait()
        second.start()
    for copy in outward:
        copy.wait()


def fused(args, groups, mc):
    dinv0, dinv1, dinv2, off0, off1, rhs0, rhs1, rhs2, list0, list1 = args
    list0, list1 = jnp.swapaxes(list0, 1, 2), jnp.swapaxes(list1, 1, 2)
    n_cols = dinv0.shape[1]
    width = rhs0.shape[1]
    mb = 2 * mc
    blocks = [d.shape[0] // mb for d in (dinv0, dinv1, dinv2)]
    high = groups[2] // groups[0]
    others = sorted(set(range(1, groups[1])) | {s * groups[0] for s in range(1, high)} | {groups[1]})
    parts = [max(k for k in (1, 2, want) if n % (2 * k) == 0) for n, want in zip(blocks, (4, 2, 2))]
    bf16, f32 = jnp.bfloat16, jnp.float32
    V = pltpu.VMEM
    r0, r1, r2 = blocks
    g0, g1, g2 = groups

    def unit(dtype, *lead):
        return V(lead + (mc, width), dtype)

    scratch = [V(a.shape, bf16) for a in (dinv0, dinv1, dinv2, off0, off1)]
    scratch += [unit(bf16, r1), unit(bf16, r2)]
    scratch += [V(a.shape[1:], jnp.int32) for a in (list0, list1)]
    scratch += [V((r0, n_cols), f32)]
    scratch += [unit(bf16, r, g) for r, g in ((r0, g0), (r1, g1), (r2, g2), (r0, g0), (r1, g1))]
    scratch += [unit(f32, r, 2) for r in (r0, r1, r2, r0, r1)]
    scratch += [unit(f32, r) for r in (r0, r1, r2, r0, r1)]
    scratch += [unit(f32, r0 // 2, 2), unit(f32, r1 // 2, 2)]
    scratch += [unit(bf16, r0 // 2, 2), unit(bf16, r1 // 2, 2)]
    scratch += [unit(bf16, r0 // 2), unit(bf16, r1 // 2)]
    scratch += [unit(bf16, r, 2) for r in (r0, r1, r2)]
    scratch += [unit(bf16, r0 // 2, 2, 2), unit(bf16, r1 // 2, 2, 2)]
    scratch += [V((width, r * mb), bf16) for r in blocks]
    top = (r2, high, g0)
    scratch += [unit(f32, r0, g0), unit(f32, r1, g1), unit(f32, *top)]
    scratch += [unit(bf16, r0, g0), unit(bf16, r1, g1), unit(bf16, *top)]
    scratch += [unit(f32, r0, g0), unit(f32, r1, g1)]
    scratch += [unit(bf16, r0, g0), unit(bf16, r1, g1)]
    scratch += [unit(bf16, g0 - 1, r0), unit(bf16, g1 - 1, r1), unit(bf16, g0 - 1, r2, high)]
    scratch += [unit(bf16, g0 - 1, r0), unit(bf16, g1 - 1, r1)]
    scratch += [unit(f32, r2, high), unit(bf16, r2, high), unit(bf16, high - 1, r2)]
    scratch += [unit(f32, r) for r in blocks]
    count = max(parts) * (4 * (g0 - 1) + 4 * (g1 - 1) + high * g0 + g0 + high + 16)
    scratch += [pltpu.SemaphoreType.DMA((count,)), pltpu.SemaphoreType.DMA((count,))]
    scratch += [pltpu.SemaphoreType.DMA((10 + sum(parts),))]
    macs = sum(d.shape[0] for d in (dinv0, dinv1, dinv2, off0, off1)) * n_cols * width
    outs = pl.pallas_call(
        functools.partial(solve_kernel, groups, blocks, parts, n_cols, mc, width, others),
        out_shape=[jax.ShapeDtypeStruct((r, mc, width), f32) for r in blocks],
        in_specs=[pl.BlockSpec(memory_space=pl.ANY)] * 10,
        out_specs=[pl.BlockSpec(memory_space=pl.ANY)] * 3,
        scratch_shapes=scratch,
        cost_estimate=pl.CostEstimate(
            flops=4 * macs, bytes_accessed=2 * macs // width, transcendentals=0
        ),
        compiler_params=pltpu.CompilerParams(
            collective_id=0, has_side_effects=True, vmem_limit_bytes=56 * 1024 * 1024
        ),
    )(
        dinv0, dinv1, dinv2, off0, off1,
        *[side.reshape(-1, mc, width) for side in (rhs0, rhs1, rhs2)],
        list0, list1,
    )
    outs = pl.pallas_call(
        hand_on,
        out_shape=[jax.ShapeDtypeStruct(out.shape, f32) for out in outs],
        in_specs=[pl.BlockSpec(memory_space=pl.ANY)] * 3,
        out_specs=[pl.BlockSpec(memory_space=pl.ANY)] * 3,
        scratch_shapes=[unit(f32, r) for r in blocks] + [pltpu.SemaphoreType.DMA((6,))],
        cost_estimate=pl.CostEstimate(
            flops=0, bytes_accessed=8 * sum(blocks) * mc * width, transcendentals=0
        ),
        compiler_params=pltpu.CompilerParams(vmem_limit_bytes=56 * 1024 * 1024),
    )(*outs)
    return tuple(out.reshape(-1, width) for out in outs)


def partner(value, axis, stride):
    return lax.ppermute(value, axis, [(i, i ^ 1 << stride) for i in range(lax.axis_size(axis))])


def own_bit(which):
    return lax.axis_index("row") >> which & 1


def row_join(pieces, depth):
    joined = pieces
    for which in range(depth):
        other = partner(joined, "row", which)
        first = jnp.concatenate((joined, other), axis=1)
        second = jnp.concatenate((other, joined), axis=1)
        joined = jnp.where(own_bit(which) == 0, first, second)
    return joined.reshape(-1, joined.shape[-1])


def row_fold(partial_value, row_blocks, depth):
    width = partial_value.shape[-1]
    folded = partial_value.reshape(row_blocks, 1 << depth, -1, width)
    for which in range(depth):
        halves = folded.reshape(row_blocks, folded.shape[1] // 2, 2, folded.shape[2], width)
        mine = own_bit(which)
        keeping = lax.dynamic_index_in_dim(halves, mine, 2, keepdims=False)
        sending = lax.dynamic_index_in_dim(halves, 1 - mine, 2, keepdims=False)
        folded = keeping + partner(sending.astype(jnp.bfloat16), "row", which).astype(sending.dtype)
    return folded


def column_sum(partial_value, col_devs, mb):
    width = partial_value.shape[-1]
    shaped = partial_value.reshape(-1, col_devs, mb // col_devs, width)
    return lax.psum_scatter(shaped, "col", scatter_dimension=1, tiled=True)


def column_join(pieces):
    gathered = lax.all_gather(pieces, "col", axis=1, tiled=True)
    return gathered.reshape(-1, gathered.shape[-1])


def sibling_fold(values, which):
    mine = own_bit(which)
    keeping = lax.dynamic_index_in_dim(values, mine, 1, keepdims=True)
    sending = lax.dynamic_index_in_dim(values, 1 - mine, 1, keepdims=True)
    return keeping + partner(sending.astype(jnp.bfloat16), "row", which).astype(sending.dtype)


def parent_rows(values, which):
    other = partner(values, "row", which)
    first = jnp.concatenate((values, other), axis=1)
    second = jnp.concatenate((other, values), axis=1)
    joined = jnp.where(own_bit(which) == 0, first, second)
    return joined.reshape(joined.shape[0] * 2, 1, joined.shape[2], joined.shape[3])


def coupling(values, listings, depth, mb):
    row_count = values.shape[0]
    row_blocks = row_count // mb
    group = 1 << depth
    position = lax.axis_index("row")
    member = position // group
    local = position % group
    owned = jnp.arange(row_blocks, dtype=jnp.int32) * group + local
    listing = lax.dynamic_index_in_dim(listings, member, 0, keepdims=False)
    listed = jnp.any(listing[None, :, :] == owned[:, None, None], axis=-1)
    unit_width = values.shape[1] // listed.shape[1]
    keeping = jnp.repeat(jnp.repeat(listed, mb, axis=0), unit_width, axis=1)
    return jnp.where(keeping, values, jnp.zeros_like(values))


def per_device(dinv0, dinv1, dinv2, offdiag0, offdiag1, rhs0, rhs1, rhs2, block_rows0, block_rows1):
    col_devs = lax.axis_size("col")
    mb = dinv0.shape[1] * col_devs // block_rows0.shape[1]
    col_width = mb // col_devs
    width = rhs0.shape[1]
    lowest_group = lax.axis_size("row") // block_rows0.shape[0]
    groups = (lowest_group, 2 * lowest_group, 4 * lowest_group)
    if col_devs == 2 and col_width % 32 == 0:
        args = (
            dinv0, dinv1, dinv2, offdiag0, offdiag1, rhs0, rhs1, rhs2, block_rows0, block_rows1
        )
        return fused(args, groups, col_width)
    depths = tuple(group.bit_length() - 1 for group in groups)
    inverses = (dinv0, dinv1, dinv2)
    couplings = (
        coupling(offdiag0, block_rows0, depths[0], mb),
        coupling(offdiag1, block_rows1, depths[1], mb),
    )
    sides = (rhs0, rhs1, rhs2)

    def as_pieces(values):
        return values.reshape(-1, 1, col_width, width)

    solved = []
    residual = as_pieces(rhs0)
    for level in range(3):
        column_form = row_join(residual, depths[level])
        product = jnp.dot(inverses[level], column_form, preferred_element_type=jnp.float32)
        solved_pieces = column_sum(product, col_devs, mb).astype(jnp.bfloat16)
        solved.append(solved_pieces)
        if level < 2:
            solved_columns = row_join(solved_pieces, depths[level])
            partial_value = jnp.dot(
                couplings[level], solved_columns, preferred_element_type=jnp.float32
            )
            summed = column_sum(partial_value, col_devs, mb)
            summed = summed.reshape(summed.shape[0] // 2, 2, col_width, width)
            update = sibling_fold(summed, depths[level])
            residual = (as_pieces(sides[level + 1]).astype(jnp.float32) - update).astype(
                jnp.bfloat16
            )
    outputs = [None, None, None]
    weighted = solved[2]
    for level in (2, 1, 0):
        row_form = column_join(weighted)
        product = jnp.einsum(
            "ij,in->jn", inverses[level], row_form, preferred_element_type=jnp.float32
        )
        answer = row_fold(product, row_form.shape[0] // mb, depths[level])
        outputs[level] = answer.reshape(-1, width)
        if level > 0:
            child_pieces = parent_rows(answer.astype(jnp.bfloat16), depths[level - 1])
            child_form = column_join(child_pieces)
            partial_value = jnp.einsum(
                "ij,in->jn", couplings[level - 1], child_form, preferred_element_type=jnp.float32
            )
            carried = row_fold(partial_value, child_form.shape[0] // mb, depths[level - 1])
            weighted = (solved[level - 1].astype(jnp.float32) - carried).astype(jnp.bfloat16)
    return (outputs[0], outputs[1], outputs[2])


def solution(mesh):
    placed = (
        P("row", "col"),
        P("row", "col"),
        P("row", "col"),
        P("row", "col"),
        P("row", "col"),
        P(("row", "col"), None),
        P(("row", "col"), None),
        P(("row", "col"), None),
        P(),
        P(),
    )
    return jax.shard_map(
        per_device,
        mesh=mesh,
        in_specs=placed,
        out_specs=(P(("row", "col"), None), P(("row", "col"), None), P(("row", "col"), None)),
        check_vma=False,
    )
```

```python
import functools

import jax
import jax.numpy as jnp
from jax import lax
from jax.experimental import pallas as pl
from jax.experimental.pallas import tpu as pltpu
from jax.sharding import PartitionSpec as P

MESH = pl.DeviceIdType.MESH


class Exchange:
    def __init__(self, send_sems, recv_sems, row, col):
        self.send_sems, self.recv_sems = send_sems, recv_sems
        self.row, self.col = row, col
        self.used = 0
        self.sent = []

    def across(self, flips):
        where = self.row
        bit = 1
        while bit <= flips:
            if flips & bit:
                where = where + (1 - 2 * (self.row // bit % 2)) * bit
            bit *= 2
        return where

    def start(self, src, dst, flips=0, other_col=False):
        col = 1 - self.col if other_col else self.col
        copy = pltpu.make_async_remote_copy(
            src_ref=src,
            dst_ref=dst,
            send_sem=self.send_sems.at[self.used],
            recv_sem=self.recv_sems.at[self.used],
            device_id=(self.across(flips), col),
            device_id_type=MESH,
        )
        self.used += 1
        copy.start()
        self.sent.append(copy)
        return copy

    def finish(self):
        for copy in self.sent:
            copy.wait_send()


def solve_kernel(
    groups, blocks, parts, n_cols, mc, width, others,
    dinv0, dinv1, dinv2, off0, off1, rhs0, rhs1, rhs2, list0, list1,
    out0, out1, out2,
    d0, d1, d2, l0, l1, b1, b2, n0, n1, mask,
    gr0, gr1, gr2, gx0, gx1,
    fp0, fp1, fp2, cp0, cp1,
    fr0, fr1, fr2, cr0, cr1,
    su0, su1, sb0, sb1, ub0, ub1,
    rw0, rw1, rw2, kw0, kw1, turned0, turned1, turned2,
    tf0, tf1, tf2, th0, th1, th2, kf0, kf1, kh0, kh1,
    tr0, tr1, tr2, kr0, kr1, zf, zh, zr, an0, an1, an2,
    send_sems, recv_sems, local_sems,
):
    row, col = lax.axis_index("row"), lax.axis_index("col")
    ex = Exchange(send_sems, recv_sems, row, col)
    mb = 2 * mc
    local = [row % g for g in groups]
    plane = groups[0]
    high = groups[2] // plane
    f32, bf16 = jnp.float32, jnp.bfloat16

    member0, member1 = row // groups[0], row // groups[1]
    pairs = [
        (rhs0, gr0.at[:, local[0]]), (dinv0, d0), (list0.at[member0], n0), (off0, l0),
        (list1.at[member1], n1), (dinv1, d1), (off1, l1), (dinv2, d2), (rhs1, b1), (rhs2, b2),
    ]
    loads = []
    for at, (src, dst) in enumerate(pairs):
        loads.append(pltpu.make_async_copy(src, dst, local_sems.at[at]))
        loads[-1].start()

    barrier = pltpu.get_barrier_semaphore()
    for flips in others:
        pl.semaphore_signal(barrier, inc=1, device_id=(ex.across(flips), col), device_id_type=MESH)
    pl.semaphore_signal(barrier, inc=1, device_id=(row, 1 - col), device_id_type=MESH)
    pl.semaphore_wait(barrier, len(others) + 1)

    def chunk(count, part, total):
        return pl.ds(part * (count // total), count // total)

    def span(level, part):
        return chunk(blocks[level], part, parts[level])

    def gather(buf, level, part):
        at = span(level, part)
        mine = buf.at[at, local[level]]
        return [ex.start(mine, mine, k) for k in range(1, groups[level])]

    def gather_top_start(buf, part):
        mine = buf.at[span(2, part), local[2]]
        along = [ex.start(mine, mine, s * plane) for s in range(1, high)]
        return along, [ex.start(mine, mine, k) for k in range(1, plane)]

    def gather_top_on(buf, part, along, waits):
        for s in range(1, high):
            along[s - 1].wait_recv()
            slot = buf.at[span(2, part), ex.across(s * plane) % groups[2]]
            waits += [ex.start(slot, slot, k) for k in range(1, plane)]

    def received(copies):
        for copy in copies:
            copy.wait_recv()

    def apply_rows(matrix, buf, prod, level, begin, count, in_part, add):
        step = min(count, 256 // mb)
        width_in = n_cols // parts[level]
        cols = pl.ds(in_part * width_in, width_in)

        def body(i, carry):
            tile = matrix[pl.ds((begin + i * step) * mb, step * mb), cols]
            form = buf[span(level, in_part)].reshape(width_in, width)
            res = jnp.dot(tile, form, preferred_element_type=f32)
            res = res.reshape(step, 2, mc, width)
            at = pl.ds(begin + i * step, step)
            prod[at] = prod[at] + res if add else res
            return carry

        lax.fori_loop(0, count // step, body, 0, unroll=True)

    def col_sum(prod, recv, at):
        return ex.start(prod.at[at, 1 - col], recv.at[at], other_col=True)

    def col_total(copy, prod, recv, at):
        copy.wait_recv()
        return prod[at, col] + recv[at]

    def build_mask(matrix, listing, level):
        count = blocks[level]
        owned = lax.broadcasted_iota(jnp.int32, (count, 1), 0) * groups[level] + local[level]
        listed = jnp.zeros((count, listing.shape[1]), f32)
        for k in range(listing.shape[0]):
            listed = listed + jnp.where(listing[k:k + 1, :] == owned, 1.0, 0.0)
        unit = lax.broadcasted_iota(jnp.int32, (listing.shape[1], n_cols), 1) // mc
        which = lax.broadcasted_iota(jnp.int32, (listing.shape[1], n_cols), 0)
        spread = jnp.where(unit == which, 1.0, 0.0).astype(bf16)
        mask[0:count, :] = jnp.dot(listed.astype(bf16), spread, preferred_element_type=f32)

        def body(i, carry):
            rows = pl.ds(i * mb, mb)
            keep = jnp.broadcast_to(mask[pl.ds(i, 1), :], (mb, n_cols)).astype(bf16)
            matrix[rows, :] = matrix[rows, :] * keep
            return carry

        lax.fori_loop(0, count, body, 0)

    def turn(form, turned, part, total):
        rows = turned.shape[1] // total
        at = chunk(form.shape[0], part, total)
        turned[:, pl.ds(part * rows, rows)] = form[at].reshape(rows, width).T

    def apply_turned(matrix, turned, prod, half, level, out_part, in_part):
        count, group = blocks[level], groups[level]
        skip = in_part * (count // parts[level] * mb)
        rows = pl.ds(skip, count * mb - skip)
        cols = max(256, mc * group)
        step = cols // (mc * group)
        tail = prod.shape[1:]

        def body(i, carry):
            begin = out_part * (n_cols // parts[level]) + i * cols
            tile = matrix[rows, pl.ds(pl.multiple_of(begin, cols), cols)]
            res = jnp.dot(turned[:, rows], tile, preferred_element_type=f32)
            res = res.T.reshape((step,) + tail)
            at = pl.ds(out_part * (count // parts[level]) + i * step, step)
            prod[at] = res
            half[at] = res.astype(bf16)
            return carry

        lax.fori_loop(0, n_cols // parts[level] // cols, body, 0, unroll=True)

    def fold(half, recv, level, part):
        group = groups[level]
        at = span(level, part)
        return [
            ex.start(half.at[at, ex.across(k) % group], recv.at[k - 1, at], k)
            for k in range(1, group)
        ]

    def folded(copies, prod, recv, level, part):
        at = span(level, part)
        total = prod[at, local[level]]
        for k, copy in enumerate(copies):
            copy.wait_recv()
            total = total + recv[k, at].astype(f32)
        return total

    def fold_top(half, recv, part):
        at = span(2, part)
        return [
            ex.start(half.at[at, :, ex.across(k) % plane], recv.at[k - 1, at], k)
            for k in range(1, plane)
        ]

    def fold_top_on(copies, prod, recv, part):
        at = span(2, part)
        total = prod[at, :, row % plane]
        for k, copy in enumerate(copies):
            copy.wait_recv()
            total = total + recv[k, at].astype(f32)
        zf[at] = total
        zh[at] = total.astype(bf16)
        return [
            ex.start(zh.at[at, ex.across(s * plane) // plane % high], zr.at[s - 1, at], s * plane)
            for s in range(1, high)
        ]

    def folded_top(copies, part):
        at = span(2, part)
        total = zf[at, row // plane % high]
        for s, copy in enumerate(copies):
            copy.wait_recv()
            total = total + zr[s, at].astype(f32)
        return total

    gathers = (gr0, gr1, gr2)
    solved = (gx0, gx1)
    inverses, couplings = (d0, d1, d2), (l0, l1)
    sides = (None, b1, b2)
    forms = (rw0, rw1, rw2)
    joins = {}

    def start_join(level, part, weighted):
        at = span(level, part)
        forms[level][at, col] = weighted
        mine = forms[level].at[at, col]
        joins[part] = ex.start(mine, mine, other_col=True)

    loads[0].wait()
    arriving = [gather(gr0, 0, part) for part in range(parts[0])]
    for at in (2, 3):
        loads[at].wait()
    build_mask(l0, n0, 0)
    loads[1].wait()
    for level in range(3):
        matrix, buf = inverses[level], gathers[level]
        prod, recv = (fp0, fp1, fp2)[level], (fr0, fr1, fr2)[level]
        size = blocks[level] // parts[level]
        spread = []
        for part in range(parts[level]):
            at, after = span(level, part), (part + 1) * size
            received(arriving[part])
            apply_rows(matrix, buf, prod, level, part * size, size, part, part > 0)
            summing = col_sum(prod, recv, at)
            if after < blocks[level]:
                apply_rows(matrix, buf, prod, level, after, blocks[level] - after, part, part > 0)
            found = col_total(summing, prod, recv, at).astype(bf16)
            if level == 2:
                start_join(2, part, found)
            else:
                solved[level][at, local[level]] = found
                spread.append(gather(solved[level], level, part))
        if level == 2:
            break
        if level == 0:
            for at in range(4, 10):
                loads[at].wait()
            build_mask(l1, n1, 1)
        matrix, buf = couplings[level], solved[level]
        prod, recv = (cp0, cp1)[level], (cr0, cr1)[level]
        last = parts[level] - 1
        for part in range(last):
            received(spread[part])
            apply_rows(matrix, buf, prod, level, 0, blocks[level], part, part > 0)
        received(spread[last])
        steps = range(parts[level + 1])
        size = blocks[level] // len(steps)
        summing = []
        for part in steps:
            apply_rows(matrix, buf, prod, level, part * size, size, last, last > 0)
            summing.append(col_sum(prod, recv, chunk(blocks[level], part, len(steps))))
        keep, away, landed = (su0, su1)[level], (sb0, sb1)[level], (ub0, ub1)[level]
        side = row // groups[level] % 2
        moving = []
        for part in steps:
            summed = col_total(
                summing[part], prod, recv, chunk(blocks[level], part, len(steps))
            )
            summed = summed.reshape(size // 2, 2, mc, width)
            at = span(level + 1, part)
            keep[at] = summed
            away[at] = summed.astype(bf16)
            moving.append(ex.start(away.at[at, 1 - side], landed.at[at], groups[level]))
        arriving = []
        for part in steps:
            moving[part].wait_recv()
            at = span(level + 1, part)
            update = keep[at, side] + landed[at].astype(f32)
            residual = (sides[level + 1][at].astype(f32) - update).astype(bf16)
            gathers[level + 1][at, local[level + 1]] = residual
            if level == 0:
                arriving.append(gather(gr1, 1, part))
            else:
                arriving.append(gather_top_start(gr2, part))
        if level == 1:
            for part in steps:
                gather_top_on(gr2, part, *arriving[part])
            arriving = [waits for _, waits in arriving]

    stored = []
    for level in (2, 1, 0):
        matrix, form, turned = inverses[level], forms[level], (turned0, turned1, turned2)[level]
        prod, half = (tf0, tf1, tf2)[level], (th0, th1, th2)[level]
        recv = (tr0, tr1, tr2)[level]
        start = fold_top if level == 2 else functools.partial(fold, level=level)
        steps = range(parts[level] - 1, -1, -1)
        moving = {}
        for part in steps:
            if level < 2:
                carried = folded(coupled[0][part], *coupled[1:], level, part)
                own = solved[level][span(level, part), local[level]].astype(f32)
                start_join(level, part, (own - carried).astype(bf16))
            joins[part].wait_recv()
            turn(form, turned, part, len(steps))
            apply_turned(matrix, turned, prod, half, level, part, part)
            moving[part] = start(half, recv, part=part)
        if level == 2:
            for part in steps:
                moving[part] = fold_top_on(moving[part], prod, recv, part)
        away, near, far = {}, {}, {}
        below = level - 1
        for part in steps:
            at = span(level, part)
            if level == 2:
                answer = folded_top(moving[part], part)
            else:
                answer = folded(moving[part], prod, recv, level, part)
            if level > 0:
                side = row // groups[below] % 2
                child = (kw0, kw1)[below]
                child[at, side, col] = answer.astype(bf16)
                mine = child.at[at, side, col]
                away[part] = ex.start(mine, mine, groups[below])
                near[part] = ex.start(mine, mine, other_col=True)
            held, out = (an0, an1, an2)[level], (out0, out1, out2)[level]
            held[at] = answer
            stored.append(
                pltpu.make_async_copy(held.at[at], out.at[at], local_sems.at[10 + len(stored)])
            )
            stored[-1].start()
        if level == 0:
            break
        for part in steps:
            away[part].wait_recv()
            theirs = child.at[span(level, part), 1 - side, col]
            far[part] = ex.start(theirs, theirs, other_col=True)
        matrix, turned = couplings[below], (turned0, turned1)[below]
        prod, half, recv = (kf0, kf1)[below], (kh0, kh1)[below], (kr0, kr1)[below]
        for part in steps:
            near[part].wait_recv()
            far[part].wait_recv()
            turn(child, turned, part, len(steps))
        moving = {}
        for part in range(parts[below] - 1, -1, -1):
            apply_turned(matrix, turned, prod, half, below, part, 0)
            moving[part] = fold(half, recv, below, part)
        coupled = (moving, prod, recv)
    for copy in stored:
        copy.wait()
    ex.finish()


def hand_on(in0, in1, in2, out0, out1, out2, held0, held1, held2, sems):
    triples = ((in0, held0, out0), (in1, held1, out1), (in2, held2, out2))
    inward = [pltpu.make_async_copy(a, b, sems.at[at]) for at, (a, b, _) in enumerate(triples)]
    outward = [
        pltpu.make_async_copy(b, c, sems.at[3 + at]) for at, (_, b, c) in enumerate(triples)
    ]
    for copy in inward:
        copy.start()
    for first, second in zip(inward, outward):
        first.wait()
        second.start()
    for copy in outward:
        copy.wait()


def fused(args, groups, mc):
    dinv0, dinv1, dinv2, off0, off1, rhs0, rhs1, rhs2, list0, list1 = args
    list0, list1 = jnp.swapaxes(list0, 1, 2), jnp.swapaxes(list1, 1, 2)
    n_cols = dinv0.shape[1]
    width = rhs0.shape[1]
    mb = 2 * mc
    blocks = [d.shape[0] // mb for d in (dinv0, dinv1, dinv2)]
    high = groups[2] // groups[0]
    others = sorted(set(range(1, groups[1])) | {s * groups[0] for s in range(1, high)} | {groups[1]})
    parts = [max(k for k in (1, 2, want) if n % (2 * k) == 0) for n, want in zip(blocks, (2, 2, 2))]
    bf16, f32 = jnp.bfloat16, jnp.float32
    V = pltpu.VMEM
    r0, r1, r2 = blocks
    g0, g1, g2 = groups

    def unit(dtype, *lead):
        return V(lead + (mc, width), dtype)

    scratch = [V(a.shape, bf16) for a in (dinv0, dinv1, dinv2, off0, off1)]
    scratch += [unit(bf16, r1), unit(bf16, r2)]
    scratch += [V(a.shape[1:], jnp.int32) for a in (list0, list1)]
    scratch += [V((r0, n_cols), f32)]
    scratch += [unit(bf16, r, g) for r, g in ((r0, g0), (r1, g1), (r2, g2), (r0, g0), (r1, g1))]
    scratch += [unit(f32, r, 2) for r in (r0, r1, r2, r0, r1)]
    scratch += [unit(f32, r) for r in (r0, r1, r2, r0, r1)]
    scratch += [unit(f32, r0 // 2, 2), unit(f32, r1 // 2, 2)]
    scratch += [unit(bf16, r0 // 2, 2), unit(bf16, r1 // 2, 2)]
    scratch += [unit(bf16, r0 // 2), unit(bf16, r1 // 2)]
    scratch += [unit(bf16, r, 2) for r in (r0, r1, r2)]
    scratch += [unit(bf16, r0 // 2, 2, 2), unit(bf16, r1 // 2, 2, 2)]
    scratch += [V((width, r * mb), bf16) for r in blocks]
    top = (r2, high, g0)
    scratch += [unit(f32, r0, g0), unit(f32, r1, g1), unit(f32, *top)]
    scratch += [unit(bf16, r0, g0), unit(bf16, r1, g1), unit(bf16, *top)]
    scratch += [unit(f32, r0, g0), unit(f32, r1, g1)]
    scratch += [unit(bf16, r0, g0), unit(bf16, r1, g1)]
    scratch += [unit(bf16, g0 - 1, r0), unit(bf16, g1 - 1, r1), unit(bf16, g0 - 1, r2, high)]
    scratch += [unit(bf16, g0 - 1, r0), unit(bf16, g1 - 1, r1)]
    scratch += [unit(f32, r2, high), unit(bf16, r2, high), unit(bf16, high - 1, r2)]
    scratch += [unit(f32, r) for r in blocks]
    count = max(parts) * (4 * (g0 - 1) + 4 * (g1 - 1) + high * g0 + g0 + high + 16)
    scratch += [pltpu.SemaphoreType.DMA((count,)), pltpu.SemaphoreType.DMA((count,))]
    scratch += [pltpu.SemaphoreType.DMA((10 + sum(parts),))]
    macs = sum(d.shape[0] for d in (dinv0, dinv1, dinv2, off0, off1)) * n_cols * width
    outs = pl.pallas_call(
        functools.partial(solve_kernel, groups, blocks, parts, n_cols, mc, width, others),
        out_shape=[jax.ShapeDtypeStruct((r, mc, width), f32) for r in blocks],
        in_specs=[pl.BlockSpec(memory_space=pl.ANY)] * 10,
        out_specs=[pl.BlockSpec(memory_space=pl.ANY)] * 3,
        scratch_shapes=scratch,
        cost_estimate=pl.CostEstimate(
            flops=4 * macs, bytes_accessed=2 * macs // width, transcendentals=0
        ),
        compiler_params=pltpu.CompilerParams(
            collective_id=0, has_side_effects=True, vmem_limit_bytes=56 * 1024 * 1024
        ),
    )(
        dinv0, dinv1, dinv2, off0, off1,
        *[side.reshape(-1, mc, width) for side in (rhs0, rhs1, rhs2)],
        list0, list1,
    )
    outs = pl.pallas_call(
        hand_on,
        out_shape=[jax.ShapeDtypeStruct(out.shape, f32) for out in outs],
        in_specs=[pl.BlockSpec(memory_space=pl.ANY)] * 3,
        out_specs=[pl.BlockSpec(memory_space=pl.ANY)] * 3,
        scratch_shapes=[unit(f32, r) for r in blocks] + [pltpu.SemaphoreType.DMA((6,))],
        cost_estimate=pl.CostEstimate(
            flops=0, bytes_accessed=8 * sum(blocks) * mc * width, transcendentals=0
        ),
        compiler_params=pltpu.CompilerParams(vmem_limit_bytes=56 * 1024 * 1024),
    )(*outs)
    return tuple(out.reshape(-1, width) for out in outs)


def partner(value, axis, stride):
    return lax.ppermute(value, axis, [(i, i ^ 1 << stride) for i in range(lax.axis_size(axis))])


def own_bit(which):
    return lax.axis_index("row") >> which & 1


def row_join(pieces, depth):
    joined = pieces
    for which in range(depth):
        other = partner(joined, "row", which)
        first = jnp.concatenate((joined, other), axis=1)
        second = jnp.concatenate((other, joined), axis=1)
        joined = jnp.where(own_bit(which) == 0, first, second)
    return joined.reshape(-1, joined.shape[-1])


def row_fold(partial_value, row_blocks, depth):
    width = partial_value.shape[-1]
    folded = partial_value.reshape(row_blocks, 1 << depth, -1, width)
    for which in range(depth):
        halves = folded.reshape(row_blocks, folded.shape[1] // 2, 2, folded.shape[2], width)
        mine = own_bit(which)
        keeping = lax.dynamic_index_in_dim(halves, mine, 2, keepdims=False)
        sending = lax.dynamic_index_in_dim(halves, 1 - mine, 2, keepdims=False)
        folded = keeping + partner(sending.astype(jnp.bfloat16), "row", which).astype(sending.dtype)
    return folded


def column_sum(partial_value, col_devs, mb):
    width = partial_value.shape[-1]
    shaped = partial_value.reshape(-1, col_devs, mb // col_devs, width)
    return lax.psum_scatter(shaped, "col", scatter_dimension=1, tiled=True)


def column_join(pieces):
    gathered = lax.all_gather(pieces, "col", axis=1, tiled=True)
    return gathered.reshape(-1, gathered.shape[-1])


def sibling_fold(values, which):
    mine = own_bit(which)
    keeping = lax.dynamic_index_in_dim(values, mine, 1, keepdims=True)
    sending = lax.dynamic_index_in_dim(values, 1 - mine, 1, keepdims=True)
    return keeping + partner(sending.astype(jnp.bfloat16), "row", which).astype(sending.dtype)


def parent_rows(values, which):
    other = partner(values, "row", which)
    first = jnp.concatenate((values, other), axis=1)
    second = jnp.concatenate((other, values), axis=1)
    joined = jnp.where(own_bit(which) == 0, first, second)
    return joined.reshape(joined.shape[0] * 2, 1, joined.shape[2], joined.shape[3])


def coupling(values, listings, depth, mb):
    row_count = values.shape[0]
    row_blocks = row_count // mb
    group = 1 << depth
    position = lax.axis_index("row")
    member = position // group
    local = position % group
    owned = jnp.arange(row_blocks, dtype=jnp.int32) * group + local
    listing = lax.dynamic_index_in_dim(listings, member, 0, keepdims=False)
    listed = jnp.any(listing[None, :, :] == owned[:, None, None], axis=-1)
    unit_width = values.shape[1] // listed.shape[1]
    keeping = jnp.repeat(jnp.repeat(listed, mb, axis=0), unit_width, axis=1)
    return jnp.where(keeping, values, jnp.zeros_like(values))


def per_device(dinv0, dinv1, dinv2, offdiag0, offdiag1, rhs0, rhs1, rhs2, block_rows0, block_rows1):
    col_devs = lax.axis_size("col")
    mb = dinv0.shape[1] * col_devs // block_rows0.shape[1]
    col_width = mb // col_devs
    width = rhs0.shape[1]
    lowest_group = lax.axis_size("row") // block_rows0.shape[0]
    groups = (lowest_group, 2 * lowest_group, 4 * lowest_group)
    if col_devs == 2 and col_width % 32 == 0:
        args = (
            dinv0, dinv1, dinv2, offdiag0, offdiag1, rhs0, rhs1, rhs2, block_rows0, block_rows1
        )
        return fused(args, groups, col_width)
    depths = tuple(group.bit_length() - 1 for group in groups)
    inverses = (dinv0, dinv1, dinv2)
    couplings = (
        coupling(offdiag0, block_rows0, depths[0], mb),
        coupling(offdiag1, block_rows1, depths[1], mb),
    )
    sides = (rhs0, rhs1, rhs2)

    def as_pieces(values):
        return values.reshape(-1, 1, col_width, width)

    solved = []
    residual = as_pieces(rhs0)
    for level in range(3):
        column_form = row_join(residual, depths[level])
        product = jnp.dot(inverses[level], column_form, preferred_element_type=jnp.float32)
        solved_pieces = column_sum(product, col_devs, mb).astype(jnp.bfloat16)
        solved.append(solved_pieces)
        if level < 2:
            solved_columns = row_join(solved_pieces, depths[level])
            partial_value = jnp.dot(
                couplings[level], solved_columns, preferred_element_type=jnp.float32
            )
            summed = column_sum(partial_value, col_devs, mb)
            summed = summed.reshape(summed.shape[0] // 2, 2, col_width, width)
            update = sibling_fold(summed, depths[level])
            residual = (as_pieces(sides[level + 1]).astype(jnp.float32) - update).astype(
                jnp.bfloat16
            )
    outputs = [None, None, None]
    weighted = solved[2]
    for level in (2, 1, 0):
        row_form = column_join(weighted)
        product = jnp.einsum(
            "ij,in->jn", inverses[level], row_form, preferred_element_type=jnp.float32
        )
        answer = row_fold(product, row_form.shape[0] // mb, depths[level])
        outputs[level] = answer.reshape(-1, width)
        if level > 0:
            child_pieces = parent_rows(answer.astype(jnp.bfloat16), depths[level - 1])
            child_form = column_join(child_pieces)
            partial_value = jnp.einsum(
                "ij,in->jn", couplings[level - 1], child_form, preferred_element_type=jnp.float32
            )
            carried = row_fold(partial_value, child_form.shape[0] // mb, depths[level - 1])
            weighted = (solved[level - 1].astype(jnp.float32) - carried).astype(jnp.bfloat16)
    return (outputs[0], outputs[1], outputs[2])


def solution(mesh):
    placed = (
        P("row", "col"),
        P("row", "col"),
        P("row", "col"),
        P("row", "col"),
        P("row", "col"),
        P(("row", "col"), None),
        P(("row", "col"), None),
        P(("row", "col"), None),
        P(),
        P(),
    )
    return jax.shard_map(
        per_device,
        mesh=mesh,
        in_specs=placed,
        out_specs=(P(("row", "col"), None), P(("row", "col"), None), P(("row", "col"), None)),
        check_vma=False,
    )
```
